256 devices in a mesh: dp: 16 (over x, z_hi, core), mp: 16 (over y, z_lo).
Axes of the slice: x: 4, y: 4, z: 8 (z_hi: 2, z_lo: 4; z = z_hi * 4 + z_lo), core: 2. Of those that a mesh axis runs over, the one named last changes fastest.
Arguments:
- weight_gate: bfloat16 [8192, 16384], P(('dp', 'mp')), may hold values from -6 to 6
- weight_up: bfloat16 [8192, 16384], P(('dp', 'mp')), may hold values from -6 to 6
- grad_gate: bfloat16 [8192, 16384], P(('dp', 'mp')), may hold values from -6 to 6
- grad_up: bfloat16 [8192, 16384], P(('dp', 'mp')), may hold values from -6 to 6
- moment_gate: bfloat16 [8192, 16384], P(('dp', 'mp')), may hold values from -4 to 4
- moment_up: bfloat16 [8192, 16384], P(('dp', 'mp')), may hold values from -4 to 4
- second_gate: bfloat16 [8192, 16384], P(('dp', 'mp')), may hold values from 0.0099487305 to 1
- second_up: bfloat16 [8192, 16384], P(('dp', 'mp')), may hold values from 0.0099487305 to 1
- layer_input: bfloat16 [4, 512, 8192], P(None, ('dp', 'mp')), may hold values from -6 to 6
- queries: bfloat16 [4, 512, 8192], P(None, ('dp', 'mp')), may hold values from -160 to 160
- fresh_keys: bfloat16 [4, 512, 1024], P(None, ('dp', 'mp')), may hold values from -16 to 16
- fresh_values: bfloat16 [4, 512, 1024], P(None, ('dp', 'mp')), may hold values from -16 to 16
- cached_keys: bfloat16 [512, 128, 1024], P(('dp', 'mp')), may hold values from -6 to 6
- cached_values: bfloat16 [512, 128, 1024], P(('dp', 'mp')), may hold values from -16 to 16
- lengths: int32 [512], P(('dp', 'mp')), may hold values from 2 to 128, as said below
- norm_gain: bfloat16 [8192], replicated, may hold values from 0.099609375 to 1.8984375
Outputs:
- gate_new: bfloat16 [8192, 16384], P('dp', 'mp')
- up_new: bfloat16 [8192, 16384], P('dp', 'mp')
- hidden: bfloat16 [4, 512, 16384], P(None, 'dp', 'mp')
The draws below stay inside these ranges and needn't reach their ends.
Inputs may be any that keep to these rules, and one draw needn't show every extreme that they name: `lengths`: every row has at least 2 cached positions and some row has exactly 128.
All inputs are finite; a program needn't handle non-finite values.
Results may differ from the reference program's by a relative error of at most 0.035.
Values may be sent and summed in bfloat16 or wider, within the bound.
No kernel may reach another device: no remote copies, remote signals or barrier semaphores. Data moves between devices by JAX's collectives and lax.ppermute only.
A program may use at most 128 MiB of HBM per device.

```python
import math
import jax
import jax.numpy as jnp
from jax import lax

D = 8192
HEADS = 64
HD = 128
KVH = 8
FW = 16384
GROUP = 8
ROWS = 512
CTX = 128
STEPS = 4
N_DP = 16


def base_keys(key):
    normals = jax.random.normal(jax.random.fold_in(key, 501), (ROWS, CTX, KVH * HD), jnp.float32)
    return jnp.clip(normals, -6.0, 6.0)


def draw_cached_keys(key, part):
    shared = base_keys(key)
    return shared.astype(jnp.bfloat16)


def draw_queries(key, part):
    key = jax.random.fold_in(key, 5)
    drawn = 1.5 * jnp.clip(jax.random.normal(key, (STEPS, ROWS, HEADS * HD), jnp.float32), -6.0, 6.0)
    return drawn.astype(jnp.bfloat16)


def draw_lengths(key, part):
    key = jax.random.fold_in(key, 7)
    filled = jax.random.randint(jax.random.fold_in(key, 1), (ROWS,), 2, CTX + 1)
    chosen = jax.random.randint(jax.random.fold_in(key, 2), (), 0, ROWS)
    return jnp.where(jnp.arange(ROWS) == chosen, CTX, filled).astype(jnp.int32)


def block_scale(own_key, shape, split, low, largest):
    loudness, own = 1.0, jax.random.fold_in(own_key, 6)
    for axis_at, parts in split:
        draws = jnp.exp(jax.random.uniform(jax.random.fold_in(own, axis_at), (parts,), jnp.float32, low / len(split), largest / len(split)))
        loudness = loudness * jnp.repeat(draws, shape[axis_at] // parts).reshape([-1 if axis == axis_at else 1 for axis in range(len(shape))])
    return loudness


def normal_values(key, extent, width, limit, cuts=(), held_as=jnp.bfloat16):
    gain = block_scale(key, extent, cuts, -0.22, 0.18) if cuts else 1.0
    entries = jax.random.normal(key, extent, jnp.float32) * width * gain
    return jnp.minimum(jnp.maximum(entries, -limit), limit).astype(held_as)


def setup_inputs(seed: int = 0) -> dict:
    key_of = jax.random.split(jax.random.key(seed), 17)
    return {
        "weight_gate": normal_values(key_of[0], (D, FW), 1.0, 6.0, ((0, 256),)),
        "weight_up": normal_values(key_of[1], (D, FW), 1.0, 6.0, ((0, 256),)),
        "grad_gate": normal_values(key_of[2], (D, FW), 1.0, 6.0, ((0, 256),)),
        "grad_up": normal_values(key_of[3], (D, FW), 1.0, 6.0, ((0, 256),)),
        "moment_gate": normal_values(key_of[4], (D, FW), 0.3, 4.0, ((0, 256),)),
        "moment_up": normal_values(key_of[5], (D, FW), 0.3, 4.0, ((0, 256),)),
        "second_gate": jnp.clip(jnp.exp(math.log(1.0) - 4.61031033 * jax.random.uniform(key_of[6], (D, FW), jnp.float32) ** block_scale(key_of[6], (D, FW), ((0, 256),), -0.2, 0.2)), 0.0099487305, 1.0).astype(jnp.bfloat16),
        "second_up": jnp.clip(jnp.exp(math.log(1.0) - 4.61031033 * jax.random.uniform(key_of[7], (D, FW), jnp.float32) ** block_scale(key_of[7], (D, FW), ((0, 256),), -0.2, 0.2)), 0.0099487305, 1.0).astype(jnp.bfloat16),
        "layer_input": normal_values(key_of[8], (STEPS, ROWS, D), 0.5, 6.0, ((1, 256),)),
        "queries": draw_queries(jax.random.fold_in(key_of[16], 71), 0),
        "fresh_keys": normal_values(key_of[10], (STEPS, ROWS, KVH * HD), 2.5, 16.0, ((1, 256),)),
        "fresh_values": normal_values(key_of[11], (STEPS, ROWS, KVH * HD), 3.0, 16.0, ((1, 256),)),
        "cached_keys": draw_cached_keys(jax.random.fold_in(key_of[16], 71), 0),
        "cached_values": normal_values(key_of[13], (ROWS, CTX, KVH * HD), 3.0, 16.0, ((0, 256),)),
        "lengths": draw_lengths(jax.random.fold_in(key_of[16], 71), 0),
        "norm_gain": jnp.clip(1.0 + 0.18 * jax.random.normal(key_of[15], (D,), jnp.float32), 0.099609375, 1.8984375).astype(jnp.bfloat16),
    }


beta_one = 0.9
beta_two = 0.95
learn_rate = 0.15
weight_decay = 0.1
adam_eps = 1e-08
first_fix = 1.0 - 0.9 ** 10
second_fix = 1.0 - 0.95 ** 10

def adamw_step(weight, gradient, moment, second):
    weight_f = weight.astype(jnp.float32)
    grad_f = gradient.astype(jnp.float32)
    moment_next = beta_one * moment.astype(jnp.float32) + (1.0 - beta_one) * grad_f
    second_next = beta_two * second.astype(jnp.float32) + (1.0 - beta_two) * grad_f * grad_f
    update = moment_next / first_fix / (jnp.sqrt(second_next / second_fix) + adam_eps)
    return (weight_f - learn_rate * (update + weight_decay * weight_f)).astype(jnp.bfloat16)

def blockwise_step(weight, gradient, moment, second):
    block_shape = (16, weight.shape[0] // 16, weight.shape[1])
    pieces_in = tuple((a.reshape(block_shape) for a in (weight, gradient, moment, second)))
    result = lax.map(lambda pieces: adamw_step(pieces[0], pieces[1], pieces[2], pieces[3]), pieces_in)
    return result.reshape(weight.shape)

def attend(query_row, fresh_k, fresh_v, cache_k, cache_v, length_row):
    row_count = query_row.shape[0]
    fresh_count = fresh_k.shape[0]
    scaled = query_row.astype(jnp.float32).reshape(row_count, KVH, GROUP, HD) * HD ** (-0.5)
    keys_old = cache_k.astype(jnp.float32).reshape(row_count, CTX, KVH, HD)
    values_old = cache_v.astype(jnp.float32).reshape(row_count, CTX, KVH, HD)
    keys_new = fresh_k.astype(jnp.float32).reshape(fresh_count, row_count, KVH, HD)
    values_new = fresh_v.astype(jnp.float32).reshape(fresh_count, row_count, KVH, HD)
    scores_old = jnp.einsum('rgjd,rpgd->rgjp', scaled, keys_old)
    visible = jnp.arange(CTX)[None, :] < length_row[:, None]
    scores_old = jnp.where(visible[:, None, None, :], scores_old, jnp.float32(-1e+30))
    scores_new = jnp.einsum('rgjd,srgd->rgjs', scaled, keys_new)
    peak_score = jnp.maximum(lax.optimization_barrier(jnp.max(scores_old, axis=-1)), lax.optimization_barrier(jnp.max(scores_new, axis=-1)))[..., None]
    exp_old = jnp.exp(scores_old - peak_score)
    exp_new = jnp.exp(scores_new - peak_score)
    totals = lax.optimization_barrier(jnp.sum(exp_old, axis=-1, keepdims=True)) + lax.optimization_barrier(jnp.sum(exp_new, axis=-1, keepdims=True))
    probs_old = lax.optimization_barrier((exp_old / totals).astype(jnp.bfloat16)).astype(jnp.float32)
    probs_new = lax.optimization_barrier((exp_new / totals).astype(jnp.bfloat16)).astype(jnp.float32)
    attended = jnp.einsum('rgjp,rpgd->rgjd', probs_old, values_old) + jnp.einsum('rgjs,srgd->rgjd', probs_new, values_new)
    return attended.reshape(row_count, KVH * GROUP * HD)

def rms_normed(residual_in, attended, norm_scale):
    summed_in = residual_in.astype(jnp.float32) + attended
    factor = lax.rsqrt(lax.optimization_barrier(jnp.mean(summed_in * summed_in, axis=-1, keepdims=True)) + 1e-06)
    return (summed_in * factor * norm_scale).astype(jnp.bfloat16)

def reference(weight_gate, weight_up, grad_gate, grad_up, moment_gate, moment_up, second_gate, second_up, layer_input, queries, fresh_keys, fresh_values, cached_keys, cached_values, lengths, norm_gain):
    gate_new = blockwise_step(weight_gate, grad_gate, moment_gate, second_gate)
    up_new = blockwise_step(weight_up, grad_up, moment_up, second_up)
    norm_scale = norm_gain.astype(jnp.float32)
    block_rows = ROWS // N_DP
    feat_block = D // N_DP
    outputs = []
    for step_idx in range(STEPS):
        fresh_count = step_idx + 1

        def one_block(pieces):
            return attend(pieces[0], pieces[1], pieces[2], pieces[3], pieces[4], pieces[5])
        query_blocks = queries[step_idx].reshape(N_DP, block_rows, HEADS * HD)
        fresh_kb = jnp.moveaxis(fresh_keys[:fresh_count].reshape(fresh_count, N_DP, block_rows, KVH * HD), 1, 0)
        fresh_vb = jnp.moveaxis(fresh_values[:fresh_count].reshape(fresh_count, N_DP, block_rows, KVH * HD), 1, 0)
        cache_kb = cached_keys.reshape(N_DP, block_rows, CTX, KVH * HD)
        cache_vb = cached_values.reshape(N_DP, block_rows, CTX, KVH * HD)
        length_b = lengths.reshape(N_DP, block_rows)
        attended = lax.map(one_block, (query_blocks, fresh_kb, fresh_vb, cache_kb, cache_vb, length_b)).reshape(ROWS, D)
        normed = rms_normed(layer_input[step_idx], attended, norm_scale)
        gate_total = jnp.zeros((ROWS, FW), jnp.float32)
        up_total = jnp.zeros((ROWS, FW), jnp.float32)
        for block_idx in range(N_DP):
            lower = block_idx * feat_block
            piece = normed[:, lower:lower + feat_block]
            gate_term = (jnp.dot(piece, gate_new[lower:lower + feat_block], preferred_element_type=jnp.float32) * D ** (-0.5)).astype(jnp.bfloat16)
            up_term = (jnp.dot(piece, up_new[lower:lower + feat_block], preferred_element_type=jnp.float32) * D ** (-0.5)).astype(jnp.bfloat16)
            gate_total = gate_total + lax.optimization_barrier(gate_term).astype(jnp.float32)
            up_total = up_total + lax.optimization_barrier(up_term).astype(jnp.float32)
        outputs.append((jax.nn.silu(gate_total) * up_total).astype(jnp.bfloat16))
    return (gate_new, up_new, jnp.stack(outputs))
```

```python
import functools

import jax
import jax.numpy as jnp
from jax import lax
from jax.experimental import pallas as pl
from jax.experimental.pallas import tpu as pltpu
from jax.sharding import PartitionSpec as P

D = 8192
HD = 128
KVH = 8
GROUP = 8
CTX = 128
STEPS = 4
ROWS_HERE = 2

GRAY = (0, 1, 3, 2)

beta_one = 0.9
beta_two = 0.95
learn_rate = 0.15
weight_decay = 0.1
adam_eps = 1e-08
first_fix = 1.0 - 0.9**10
second_fix = 1.0 - 0.95**10


def dp_swap(flip_x, flip_z, flip_core):
    pairs = []
    for dp in range(16):
        x, z_hi, core = dp // 4, dp // 2 % 2, dp % 2
        x_to = GRAY[GRAY[x] ^ flip_x]
        pairs.append((dp, x_to * 4 + (z_hi ^ flip_z) * 2 + (core ^ flip_core)))
    return pairs


def mp_swap(flip_y, flip_z):
    pairs = []
    for mp in range(16):
        y, z_lo = mp // 4, mp % 4
        pairs.append((mp, GRAY[GRAY[y] ^ flip_y] * 4 + (z_lo ^ flip_z)))
    return pairs


def adam_kernel(weight_ref, grad_ref, moment_ref, second_ref, out_ref):
    width = out_ref.shape[2]
    for part in range(out_ref.shape[0]):
        cols = slice(part * width, (part + 1) * width)
        weight_f = weight_ref[:, cols].astype(jnp.float32)
        grad_f = grad_ref[:, cols].astype(jnp.float32)
        moment_next = (
            beta_one * moment_ref[:, cols].astype(jnp.float32) + (1.0 - beta_one) * grad_f
        )
        second_next = (
            beta_two * second_ref[:, cols].astype(jnp.float32)
            + (1.0 - beta_two) * grad_f * grad_f
        )
        update = moment_next / first_fix / (jnp.sqrt(second_next / second_fix) + adam_eps)
        new = weight_f - learn_rate * (update + weight_decay * weight_f)
        out_ref[part] = new.astype(jnp.bfloat16)


def adam_blocks(weight, gradient, moment, second):
    rows, cols = weight.shape
    width = cols // 16
    per_step = 2
    spec = pl.BlockSpec((rows, per_step * width), lambda i: (0, i))
    return pl.pallas_call(
        adam_kernel,
        grid=(16 // per_step,),
        in_specs=[spec] * 4,
        out_specs=pl.BlockSpec((per_step, rows, width), lambda i: (i, 0, 0)),
        out_shape=jax.ShapeDtypeStruct((16, rows, width), jnp.bfloat16),
        cost_estimate=pl.CostEstimate(
            flops=20 * rows * cols, bytes_accessed=10 * rows * cols, transcendentals=2 * rows * cols
        ),
        name="adam",
    )(weight, gradient, moment, second)


def attend_all(queries, fresh_keys, fresh_values, cached_keys, cached_values, lengths):
    q = queries.reshape(STEPS, ROWS_HERE, KVH, GROUP, HD)
    keys_old = cached_keys.reshape(ROWS_HERE, CTX, KVH, HD)
    values_old = cached_values.reshape(ROWS_HERE, CTX, KVH, HD)
    keys_new = fresh_keys.reshape(STEPS, ROWS_HERE, KVH, HD)
    values_new = fresh_values.reshape(STEPS, ROWS_HERE, KVH, HD)
    scale = HD ** (-0.5)
    scores_old = scale * jnp.einsum(
        "srgjd,rpgd->rgsjp", q, keys_old, preferred_element_type=jnp.float32
    )
    scores_new = scale * jnp.einsum(
        "srgjd,trgd->rgsjt", q, keys_new, preferred_element_type=jnp.float32
    )
    visible = jnp.arange(CTX)[None, :] < lengths[:, None]
    scores_old = jnp.where(visible[:, None, None, None, :], scores_old, jnp.float32(-1e30))
    causal = jnp.arange(STEPS)[None, :] <= jnp.arange(STEPS)[:, None]
    scores_new = jnp.where(causal[None, None, :, None, :], scores_new, jnp.float32(-1e30))
    peak = jnp.maximum(jnp.max(scores_old, axis=-1), jnp.max(scores_new, axis=-1))[..., None]
    exp_old = jnp.exp(scores_old - peak)
    exp_new = jnp.exp(scores_new - peak)
    totals = jnp.sum(exp_old, axis=-1, keepdims=True) + jnp.sum(exp_new, axis=-1, keepdims=True)
    probs_old = (exp_old / totals).astype(jnp.bfloat16)
    probs_new = (exp_new / totals).astype(jnp.bfloat16)
    attended = jnp.einsum(
        "rgsjp,rpgd->srgjd", probs_old, values_old, preferred_element_type=jnp.float32
    ) + jnp.einsum("rgsjt,trgd->srgjd", probs_new, values_new, preferred_element_type=jnp.float32)
    return attended.reshape(STEPS, ROWS_HERE, D)


def product_kernel(chip_ref, *refs):
    row_refs = refs[:4]
    own_ref, other_ref, send_a, keep_a, send_b, keep_b = refs[4:]
    half = own_ref.shape[1] // 2
    depth = own_ref.shape[0]
    gray_here, z_here = chip_ref[0], chip_ref[1]
    for flip in (3, 1, 2, 0):
        gray = gray_here ^ flip
        x = gray ^ (gray >> 1)
        rows = jnp.concatenate(
            [ref[x * 2 + (z_here ^ flip_z)] for flip_z in range(2) for ref in row_refs], axis=0
        )
        total = jnp.dot(rows[:, :depth], own_ref[...], preferred_element_type=jnp.float32)
        total += jnp.dot(rows[:, depth:], other_ref[...], preferred_element_type=jnp.float32)
        term = (total * D ** (-0.5)).astype(jnp.bfloat16).reshape(2, 128, 2 * half)
        (send_a if flip & 1 else keep_a)[flip >> 1] = term[:, :, :half]
        (send_b if flip & 2 else keep_b)[flip & 1] = term[:, :, half:]


def products(chip, row_parts, own, other):
    half = own.shape[1] // 2
    out = jax.ShapeDtypeStruct((2, 2, 128, half), jnp.bfloat16)
    vmem = pl.BlockSpec(memory_space=pltpu.VMEM)
    return pl.pallas_call(
        product_kernel,
        in_specs=[pl.BlockSpec(memory_space=pltpu.SMEM)] + [vmem] * 6,
        out_specs=[vmem] * 4,
        out_shape=[out] * 4,
        compiler_params=pltpu.CompilerParams(vmem_limit_bytes=32 * 2**20),
        cost_estimate=pl.CostEstimate(
            flops=2 * 1024 * 1024 * 1024, bytes_accessed=6 * 2**20, transcendentals=0
        ),
        name="products",
    )(chip, *row_parts, own, other)


def add(kept, arrived):
    return kept.astype(jnp.float32) + arrived.astype(jnp.float32)


def scatter_sums(parts):
    send_a, keep_a, send_b, keep_b = parts
    got_a = lax.ppermute(send_a, "dp", dp_swap(1, 0, 0))
    got_b = lax.ppermute(send_b, "dp", dp_swap(2, 0, 0))
    sum_a = add(keep_a, got_a)
    sum_b = add(keep_b, got_b)
    got_a = lax.ppermute(sum_a[1].astype(jnp.bfloat16), "dp", dp_swap(2, 0, 0))
    got_b = lax.ppermute(sum_b[1].astype(jnp.bfloat16), "dp", dp_swap(1, 0, 0))
    sum_a = add(sum_a[0], got_a)
    sum_b = add(sum_b[0], got_b)
    both = jnp.concatenate([sum_a, sum_b], axis=-1)
    got = lax.ppermute(both[1].astype(jnp.bfloat16), "dp", dp_swap(0, 1, 0))
    return add(both[0], got)


def local(
    weight_gate,
    weight_up,
    grad_gate,
    grad_up,
    moment_gate,
    moment_up,
    second_gate,
    second_up,
    layer_input,
    queries,
    fresh_keys,
    fresh_values,
    cached_keys,
    cached_values,
    lengths,
    norm_gain,
):
    dp = lax.axis_index("dp")
    mp = lax.axis_index("mp")
    x, z_hi, core = dp // 4, dp // 2 % 2, dp % 2
    y, z_lo = mp // 4, mp % 4
    chip = jnp.stack([x ^ (x >> 1), z_hi]).astype(jnp.int32)

    attended = attend_all(
        queries, fresh_keys, fresh_values, cached_keys, cached_values, lengths
    )
    summed_in = layer_input.astype(jnp.float32) + attended
    factor = lax.rsqrt(jnp.mean(summed_in * summed_in, axis=-1, keepdims=True) + 1e-06)
    normed = (summed_in * factor * norm_gain.astype(jnp.float32)).astype(jnp.bfloat16)
    halves = normed.reshape(8, 8, 2, 512).transpose(1, 2, 0, 3)
    halves = jnp.where(core == 0, halves, halves[:, ::-1])
    blocks = halves.transpose(0, 2, 1, 3).reshape(8, 8, 1024)
    gate_step = adam_blocks(weight_gate, grad_gate, moment_gate, second_gate)
    up_step = adam_blocks(weight_up, grad_up, moment_up, second_up)

    groups = [[2 * chip_at + kind for chip_at in range(8)] for kind in range(2)]
    spread = lax.all_to_all(
        blocks, "dp", split_axis=0, concat_axis=0, axis_index_groups=groups, tiled=True
    )
    along_z = [spread] + [lax.ppermute(spread, "mp", mp_swap(0, k)) for k in (1, 2, 3)]
    column = jnp.concatenate(along_z, axis=1)
    row_parts = [column] + [lax.ppermute(column, "mp", mp_swap(k, 0)) for k in (1, 2, 3)]

    news, totals = [], []
    for step in (gate_step, up_step):
        new = lax.all_to_all(step, "mp", split_axis=0, concat_axis=0, tiled=True)
        new = new.reshape(512, 1024)
        other = lax.ppermute(new, "dp", dp_swap(0, 0, 1))
        news.append(new)
        totals.append(scatter_sums(products(chip, row_parts, new, other)))
    gate_total, up_total = totals
    hidden = (jax.nn.silu(gate_total) * up_total).astype(jnp.bfloat16)

    at = jnp.arange(128)
    y_flip, z_flip, step_at, row_at = at // 32, at // 8 % 4, at // 2 % 4, at % 2
    gray_from = (y ^ (y >> 1)) ^ y_flip
    y_from = gray_from ^ (gray_from >> 1)
    target = step_at * 32 + (y_from * 4 + (z_lo ^ z_flip)) * 2 + row_at
    placed = (at[:, None] == target[None, :]).astype(jnp.bfloat16)
    hidden = jnp.dot(placed, hidden, preferred_element_type=jnp.float32).astype(jnp.bfloat16)
    return news[0], news[1], hidden.reshape(STEPS, 32, 1024)


def solution(mesh):
    rows = P(("dp", "mp"), None)
    steps = P(None, ("dp", "mp"), None)
    cache = P(("dp", "mp"), None, None)
    in_specs = (rows,) * 8 + (steps,) * 4 + (cache,) * 2 + (P(("dp", "mp")), P())
    out_specs = (P("dp", "mp"), P("dp", "mp"), P(None, "dp", "mp"))
    return jax.shard_map(local, mesh=mesh, in_specs=in_specs, out_specs=out_specs, check_vma=False)
```

```python
import jax
import jax.numpy as jnp
from jax import lax
from jax.experimental import pallas as pl
from jax.experimental.pallas import tpu as pltpu
from jax.sharding import PartitionSpec as P

D = 8192
HD = 128
KVH = 8
GROUP = 8
CTX = 128
STEPS = 4
ROWS_HERE = 2

BRIEF = pl.CostEstimate(flops=1, bytes_accessed=1, transcendentals=0)

GRAY = (0, 1, 3, 2)

beta_one = 0.9
beta_two = 0.95
learn_rate = 0.15
weight_decay = 0.1
adam_eps = 1e-08
first_fix = 1.0 - 0.9**10
second_fix = 1.0 - 0.95**10


def dp_swap(flip_x, flip_z, flip_core):
    pairs = []
    for dp in range(16):
        x, z_hi, core = dp // 4, dp // 2 % 2, dp % 2
        x_to = GRAY[GRAY[x] ^ flip_x]
        pairs.append((dp, x_to * 4 + (z_hi ^ flip_z) * 2 + (core ^ flip_core)))
    return pairs


def mp_swap(flip_y, flip_z):
    pairs = []
    for mp in range(16):
        y, z_lo = mp // 4, mp % 4
        pairs.append((mp, GRAY[GRAY[y] ^ flip_y] * 4 + (z_lo ^ flip_z)))
    return pairs


def adam_kernel(weight_ref, grad_ref, moment_ref, second_ref, cols):
    weight_f = weight_ref[:, cols].astype(jnp.float32)
    grad_f = grad_ref[:, cols].astype(jnp.float32)
    moment_f = moment_ref[:, cols].astype(jnp.float32)
    second_f = second_ref[:, cols].astype(jnp.float32)
    rise = (learn_rate * beta_one / first_fix) * moment_f
    rise += (learn_rate * (1.0 - beta_one) / first_fix) * grad_f
    spread = (beta_two / second_fix) * second_f
    spread += ((1.0 - beta_two) / second_fix) * (grad_f * grad_f)
    root = spread * lax.rsqrt(spread) + adam_eps
    new = (1.0 - learn_rate * weight_decay) * weight_f - rise * lax.rsqrt(root * root)
    return new.astype(jnp.bfloat16)


def adam_places_kernel(*refs):
    *in_refs, out_ref = refs
    width = out_ref.shape[2]
    for part in range(out_ref.shape[0]):
        out_ref[part] = adam_kernel(*in_refs, slice(part * width, (part + 1) * width))


def adam_places(*arrays):
    rows, cols = arrays[0].shape
    width = cols // 16
    return pl.pallas_call(
        adam_places_kernel,
        grid=(4,),
        in_specs=[pl.BlockSpec((rows, 4 * width), lambda i: (0, i))] * 4,
        out_specs=pl.BlockSpec((4, rows, width), lambda i: (i, 0, 0)),
        out_shape=jax.ShapeDtypeStruct((16, rows, width), jnp.bfloat16),
        cost_estimate=BRIEF,
        name="adam_places",
    )(*arrays)


def adam_flips_kernel(at_ref, *refs):
    in_refs, out_refs = refs[:4], refs[4:]
    width = out_refs[0].shape[2]
    for flip in range(4):
        cols = pl.ds(pl.multiple_of((at_ref[4] ^ flip) * width, width), width)
        new = adam_kernel(*in_refs, cols)
        for y_flip, out_ref in enumerate(out_refs):

            @pl.when(pl.program_id(0) == y_flip)
            def _():
                out_ref[flip] = new


def adam_flips(at, *arrays):
    rows, cols = arrays[0].shape
    width = cols // 16
    return pl.pallas_call(
        adam_flips_kernel,
        grid_spec=pltpu.PrefetchScalarGridSpec(
            num_scalar_prefetch=1,
            grid=(4,),
            in_specs=[pl.BlockSpec((rows, 4 * width), lambda i, at: (0, at[i]))] * 4,
            out_specs=[pl.BlockSpec((4, rows, width), lambda i, at: (0, 0, 0))] * 4,
        ),
        out_shape=[jax.ShapeDtypeStruct((4, rows, width), jnp.bfloat16)] * 4,
        cost_estimate=BRIEF,
        name="adam_flips",
    )(at, *arrays)


def whole(kernel, out_shape, name, scalars, *arrays):
    vmem = pl.BlockSpec(memory_space=pltpu.VMEM)
    return pl.pallas_call(
        kernel,
        in_specs=[pl.BlockSpec(memory_space=pltpu.SMEM)] * len(scalars) + [vmem] * len(arrays),
        out_specs=jax.tree.map(lambda _: vmem, out_shape),
        out_shape=out_shape,
        compiler_params=pltpu.CompilerParams(vmem_limit_bytes=20 * 2**20),
        cost_estimate=BRIEF,
        name=name,
    )(*scalars, *arrays)


def regroup_kernel(*refs):
    for outer in range(4):
        for inner in range(4):
            refs[4 + inner][outer] = refs[outer][inner]


def regroup(parts):
    out = [jax.ShapeDtypeStruct(parts[0].shape, parts[0].dtype)] * 4
    return whole(regroup_kernel, out, "regroup", (), *parts)


def assemble_into(out_ref, at_ref, *refs):
    rows = refs[0].shape[1]
    for z_flip in range(4):
        for y_flip in range(4):
            source = at_ref[y_flip] * 4 + (at_ref[4] ^ z_flip)
            place = pl.ds(pl.multiple_of(source * rows, rows), rows)
            out_ref[place] = refs[z_flip][y_flip]


def swap_axes_kernel(*refs):
    for flip in range(4):
        for flip_z in range(2):
            refs[4 + flip_z][flip] = refs[flip][flip_z]


def swap_axes(parts):
    out = [jax.ShapeDtypeStruct((4, *parts[0].shape[1:]), parts[0].dtype)] * 2
    return whole(swap_axes_kernel, out, "swap", (), *parts)


def interleave_kernel(first_ref, second_ref, out_ref):
    for flip in range(4):
        out_ref[2 * flip] = first_ref[flip]
        out_ref[2 * flip + 1] = second_ref[flip]


def interleave(first, second):
    out = jax.ShapeDtypeStruct((8, *first.shape[1:]), first.dtype)
    return whole(interleave_kernel, out, "interleave", (), first, second)


def column_kernel(*refs):
    for at in range(refs[-1].shape[0]):
        rows = [ref[at].astype(jnp.float32) for ref in refs[:-1]]
        refs[-1][at] = jnp.concatenate(rows, axis=0).astype(jnp.bfloat16)


def join_rows(parts):
    blocks, rows, width = parts[0].shape
    out = jax.ShapeDtypeStruct((blocks, len(parts) * rows, width), parts[0].dtype)
    return whole(column_kernel, out, "column", (), *parts)


def attend_kernel(
    to_ref, lengths_ref, query_ref, input_ref, new_k_ref, new_v_ref, old_k_ref, old_v_ref,
    gain_ref, *refs,
):
    *out_refs, summed_ref, normed_ref = refs
    rows = STEPS * ROWS_HERE
    stacked = GROUP * rows

    def flat(ref):
        return ref[...].astype(jnp.float32).reshape(rows, ref.shape[2])

    queries, new_k, new_v = flat(query_ref), flat(new_k_ref), flat(new_v_ref)
    new_k, new_v = new_k.astype(jnp.bfloat16), new_v.astype(jnp.bfloat16)
    at = lax.broadcasted_iota(jnp.int32, (stacked, CTX), 0)
    position = lax.broadcasted_iota(jnp.int32, (stacked, CTX), 1)
    first_row = at % ROWS_HERE == 0
    visible = position < jnp.where(first_row, lengths_ref[0], lengths_ref[1])
    at_new = lax.broadcasted_iota(jnp.int32, (stacked, rows), 0)
    key_new = lax.broadcasted_iota(jnp.int32, (stacked, rows), 1)
    visible_new = (key_new % ROWS_HERE == at_new % ROWS_HERE) & (
        key_new // ROWS_HERE <= at_new // ROWS_HERE % STEPS
    )

    def scores(query, keys):
        found = lax.dot_general(
            query, keys, (((1,), (1,)), ((), ())), preferred_element_type=jnp.float32
        )
        return found * HD ** (-0.5)

    def weighted(probs, values):
        return jnp.dot(probs, values, preferred_element_type=jnp.float32)

    squares = jnp.zeros((rows, HD), jnp.float32)
    for group in range(KVH):
        cols = slice(group * HD, (group + 1) * HD)
        heads = [
            slice((group * GROUP + j) * HD, (group * GROUP + j + 1) * HD) for j in range(GROUP)
        ]
        query = jnp.concatenate([queries[:, head] for head in heads], axis=0).astype(jnp.bfloat16)
        old = jnp.where(
            first_row, scores(query, old_k_ref[0, :, cols]), scores(query, old_k_ref[1, :, cols])
        )
        old = jnp.where(visible, old, -1e30)
        new = jnp.where(visible_new, scores(query, new_k[:, cols]), -1e30)
        peak = jnp.maximum(
            jnp.max(old, axis=1, keepdims=True), jnp.max(new, axis=1, keepdims=True)
        )
        old, new = jnp.exp(old - peak), jnp.exp(new - peak)
        total = jnp.sum(old, axis=1, keepdims=True) + jnp.sum(new, axis=1, keepdims=True)
        old, new = old / total, new / total
        attended = weighted(
            jnp.where(first_row, old, 0.0).astype(jnp.bfloat16), old_v_ref[0, :, cols]
        )
        attended += weighted(
            jnp.where(first_row, 0.0, old).astype(jnp.bfloat16), old_v_ref[1, :, cols]
        )
        attended += weighted(new.astype(jnp.bfloat16), new_v[:, cols])
        for j, head in enumerate(heads):
            part = input_ref[:, :, head].astype(jnp.float32).reshape(rows, HD)
            part += attended[j * rows : (j + 1) * rows]
            summed_ref[:, head] = part
            squares += part * part
    factor = lax.rsqrt(jnp.sum(squares, axis=1, keepdims=True) / D + 1e-06)
    for block in range(8):
        cols = slice(block * 1024, (block + 1) * 1024)
        gain = gain_ref[:, cols].astype(jnp.float32)
        normed_ref[block] = summed_ref[:, cols] * factor * gain
    mine = pl.ds(pl.multiple_of(to_ref[8] * 512, 512), 512)
    its = pl.ds(pl.multiple_of((1 - to_ref[8]) * 512, 512), 512)
    for flip, out_ref in enumerate(out_refs):
        for flip_z in range(2):
            chip = to_ref[2 * flip + flip_z]
            out_ref[flip_z, :, :512] = normed_ref[chip, :, mine].astype(jnp.bfloat16)
            out_ref[flip_z, :, 512:] = normed_ref[chip, :, its].astype(jnp.bfloat16)


def attend(to, lengths, *arrays):
    rows = STEPS * ROWS_HERE
    smem, vmem = pl.BlockSpec(memory_space=pltpu.SMEM), pl.BlockSpec(memory_space=pltpu.VMEM)
    return pl.pallas_call(
        attend_kernel,
        in_specs=[smem] * 2 + [vmem] * len(arrays),
        out_specs=[vmem] * 4,
        out_shape=[jax.ShapeDtypeStruct((2, rows, 1024), jnp.bfloat16)] * 4,
        scratch_shapes=[
            pltpu.VMEM((rows, D), jnp.float32),
            pltpu.VMEM((8, rows, 1024), jnp.float32),
        ],
        compiler_params=pltpu.CompilerParams(vmem_limit_bytes=12 * 2**20),
        cost_estimate=BRIEF,
        name="attend",
    )(to, lengths, *arrays)


def product_kernel(*refs):
    row_refs = refs[:4]
    own_ref, other_ref, send_a, keep_a, send_b, keep_b, new_ref = refs[4:]
    new_ref[...] = own_ref[...]
    half = own_ref.shape[1] // 2
    depth = own_ref.shape[0]
    for flip in (3, 1, 2, 0):
        rows = jnp.concatenate(
            [ref[2 * flip + flip_z] for flip_z in range(2) for ref in row_refs], axis=0
        )
        total = jnp.dot(rows[:, :depth], own_ref[...], preferred_element_type=jnp.float32)
        total += jnp.dot(rows[:, depth:], other_ref[...], preferred_element_type=jnp.float32)
        term = (total * D ** (-0.5)).astype(jnp.bfloat16).reshape(2, 128, 2 * half)
        (send_a if flip & 1 else keep_a)[flip >> 1] = term[:, :, :half]
        (send_b if flip & 2 else keep_b)[flip & 1] = term[:, :, half:]


def product_kernel_and_next(at_ref, *refs):
    *refs, next_ref = refs
    assemble_into(next_ref, at_ref, *refs[6:10])
    product_kernel(*refs[:6], *refs[10:])


def products(row_parts, own, other, at=None, next_parts=()):
    half = own.shape[1] // 2
    out = jax.ShapeDtypeStruct((2, 2, 128, half), jnp.bfloat16)
    whole_own = jax.ShapeDtypeStruct(own.shape, own.dtype)
    arrays = (*row_parts, own, other, *next_parts)
    if next_parts:
        return whole(
            product_kernel_and_next, [out] * 4 + [whole_own] * 2, "products", (at,), *arrays
        )
    return whole(product_kernel, [out] * 4 + [whole_own], "products", (), *arrays)


def add(kept, arrived):
    return kept.astype(jnp.float32) + arrived.astype(jnp.float32)


def over_z(parts):
    return [parts[0]] + [lax.ppermute(parts[k], "mp", mp_swap(0, k)) for k in (1, 2, 3)]


def over_y(parts):
    return [parts[0]] + [lax.ppermute(parts[k], "mp", mp_swap(k, 0)) for k in (1, 2, 3)]


def swap_core(own):
    return lax.ppermute(own, "dp", dp_swap(0, 0, 1))


def first_sums(parts):
    send_a, keep_a, send_b, keep_b = parts
    got_a = lax.ppermute(send_a, "dp", dp_swap(1, 0, 0))
    got_b = lax.ppermute(send_b, "dp", dp_swap(2, 0, 0))
    return add(keep_a, got_a), add(keep_b, got_b)


def second_sums(sum_a, sum_b):
    got_a = lax.ppermute(sum_a[1].astype(jnp.bfloat16), "dp", dp_swap(2, 0, 0))
    got_b = lax.ppermute(sum_b[1].astype(jnp.bfloat16), "dp", dp_swap(1, 0, 0))
    return jnp.concatenate([add(sum_a[0], got_a), add(sum_b[0], got_b)], axis=-1)


def last_sum(both):
    return add(both[0], lax.ppermute(both[1].astype(jnp.bfloat16), "dp", dp_swap(0, 1, 0)))


def local(
    weight_gate,
    weight_up,
    grad_gate,
    grad_up,
    moment_gate,
    moment_up,
    second_gate,
    second_up,
    layer_input,
    queries,
    fresh_keys,
    fresh_values,
    cached_keys,
    cached_values,
    lengths,
    norm_gain,
):
    dp = lax.axis_index("dp")
    mp = lax.axis_index("mp")
    x, z_hi, core = dp // 4, dp // 2 % 2, dp % 2
    y, z_lo = mp // 4, mp % 4
    gray_x, gray_y = x ^ (x >> 1), y ^ (y >> 1)

    def place(gray):
        return gray ^ (gray >> 1)

    at = jnp.stack([place(gray_y ^ flip) for flip in range(4)] + [z_lo]).astype(jnp.int32)
    to = jnp.stack(
        [place(gray_x ^ flip) * 2 + (z_hi ^ flip_z) for flip in range(4) for flip_z in range(2)]
        + [core]
    ).astype(jnp.int32)

    gate_step = adam_places(weight_gate, grad_gate, moment_gate, second_gate)
    gate_step, queries = lax.optimization_barrier((gate_step, queries))
    gate_own = lax.all_to_all(gate_step, "mp", split_axis=0, concat_axis=0, tiled=True)
    gate_own = gate_own.reshape(512, 1024)

    by_x = attend(
        to, lengths, queries, layer_input, fresh_keys, fresh_values, cached_keys, cached_values,
        norm_gain.reshape(1, D),
    )
    by_x, weight_up = lax.optimization_barrier((by_x, weight_up))
    up_parts = adam_flips(at, weight_up, grad_up, moment_up, second_up)
    by_x, up_parts = lax.optimization_barrier((by_x, up_parts))
    up_parts = over_y(up_parts)
    by_x = [by_x[0]] + [lax.ppermute(by_x[k], "dp", dp_swap(k, 0, 0)) for k in (1, 2, 3)]
    here, there = swap_axes(by_x)
    spread = interleave(here, lax.ppermute(there, "dp", dp_swap(0, 1, 0)))
    along_z = over_z([spread] * 4)
    column, up_parts, gate_own = lax.optimization_barrier(
        (join_rows(along_z), up_parts, gate_own)
    )
    gate_other = swap_core(gate_own)
    row_parts = over_y([column] * 4)
    up_parts = over_z(regroup(up_parts))
    *gate_terms, gate_new, up_own = products(row_parts, gate_own, gate_other, at, up_parts)
    *up_terms, up_new = products(row_parts, up_own, swap_core(up_own))

    gate_terms[1], gate_terms[3], up_new = lax.optimization_barrier(
        (gate_terms[1], gate_terms[3], up_new)
    )
    gate_both = second_sums(*first_sums(gate_terms))
    up_both = second_sums(*first_sums(up_terms))
    gate_total, up_both = lax.optimization_barrier((last_sum(gate_both), up_both))
    up_total = last_sum(up_both)
    hidden = (jax.nn.silu(gate_total) * up_total).astype(jnp.bfloat16)

    row = jnp.arange(128)
    y_flip, z_flip, step_at, row_at = row // 32, row // 8 % 4, row // 2 % 4, row % 2
    target = step_at * 32 + (place(gray_y ^ y_flip) * 4 + (z_lo ^ z_flip)) * 2 + row_at
    placed = (row[:, None] == target[None, :]).astype(jnp.bfloat16)
    hidden = jnp.dot(placed, hidden, preferred_element_type=jnp.float32).astype(jnp.bfloat16)
    return gate_new, up_new, hidden.reshape(STEPS, 32, 1024)


def solution(mesh):
    rows = P(("dp", "mp"), None)
    steps = P(None, ("dp", "mp"), None)
    cache = P(("dp", "mp"), None, None)
    in_specs = (rows,) * 8 + (steps,) * 4 + (cache,) * 2 + (P(("dp", "mp")), P())
    out_specs = (P("dp", "mp"), P("dp", "mp"), P(None, "dp", "mp"))
    return jax.shard_map(local, mesh=mesh, in_specs=in_specs, out_specs=out_specs, check_vma=False)
```

```python
import jax
import jax.numpy as jnp
from jax import lax
from jax.experimental import pallas as pl
from jax.experimental.pallas import tpu as pltpu
from jax.sharding import PartitionSpec as P

D = 8192
HD = 128
KVH = 8
GROUP = 8
CTX = 128
STEPS = 4
ROWS_HERE = 2

BRIEF = pl.CostEstimate(flops=1, bytes_accessed=1, transcendentals=0)

GRAY = (0, 1, 3, 2)

beta_one = 0.9
beta_two = 0.95
learn_rate = 0.15
weight_decay = 0.1
adam_eps = 1e-08
first_fix = 1.0 - 0.9**10
second_fix = 1.0 - 0.95**10


def dp_swap(flip_x, flip_z, flip_core):
    pairs = []
    for dp in range(16):
        x, z_hi, core = dp // 4, dp // 2 % 2, dp % 2
        x_to = GRAY[GRAY[x] ^ flip_x]
        pairs.append((dp, x_to * 4 + (z_hi ^ flip_z) * 2 + (core ^ flip_core)))
    return pairs


def mp_swap(flip_y, flip_z):
    pairs = []
    for mp in range(16):
        y, z_lo = mp // 4, mp % 4
        pairs.append((mp, GRAY[GRAY[y] ^ flip_y] * 4 + (z_lo ^ flip_z)))
    return pairs


def adam_kernel(weight_ref, grad_ref, moment_ref, second_ref, cols):
    weight_f = weight_ref[:, cols].astype(jnp.float32)
    grad_f = grad_ref[:, cols].astype(jnp.float32)
    moment_f = moment_ref[:, cols].astype(jnp.float32)
    second_f = second_ref[:, cols].astype(jnp.float32)
    rise = (learn_rate * beta_one / first_fix) * moment_f
    rise += (learn_rate * (1.0 - beta_one) / first_fix) * grad_f
    spread = (beta_two / second_fix) * second_f
    spread += ((1.0 - beta_two) / second_fix) * (grad_f * grad_f)
    root = spread * lax.rsqrt(spread) + adam_eps
    new = (1.0 - learn_rate * weight_decay) * weight_f - rise * lax.rsqrt(root * root)
    return new.astype(jnp.bfloat16)


def adam_places_kernel(*refs):
    *in_refs, out_ref = refs
    width = out_ref.shape[2]
    for part in range(out_ref.shape[0]):
        out_ref[part] = adam_kernel(*in_refs, slice(part * width, (part + 1) * width))


def adam_places(*arrays):
    rows, cols = arrays[0].shape
    width = cols // 16
    return pl.pallas_call(
        adam_places_kernel,
        grid=(4,),
        in_specs=[pl.BlockSpec((rows, 4 * width), lambda i: (0, i))] * 4,
        out_specs=pl.BlockSpec((4, rows, width), lambda i: (i, 0, 0)),
        out_shape=jax.ShapeDtypeStruct((16, rows, width), jnp.bfloat16),
        cost_estimate=BRIEF,
        name="adam_places",
    )(*arrays)


def adam_flips_kernel(at_ref, *refs):
    in_refs, out_refs = refs[:4], refs[4:]
    width = out_refs[0].shape[2]
    for flip in range(4):
        cols = pl.ds(pl.multiple_of((at_ref[4] ^ flip) * width, width), width)
        new = adam_kernel(*in_refs, cols)
        for y_flip, out_ref in enumerate(out_refs):

            @pl.when(pl.program_id(0) == y_flip)
            def _():
                out_ref[flip] = new


def adam_flips(at, *arrays):
    rows, cols = arrays[0].shape
    width = cols // 16
    return pl.pallas_call(
        adam_flips_kernel,
        grid_spec=pltpu.PrefetchScalarGridSpec(
            num_scalar_prefetch=1,
            grid=(4,),
            in_specs=[pl.BlockSpec((rows, 4 * width), lambda i, at: (0, at[i]))] * 4,
            out_specs=[pl.BlockSpec((4, rows, width), lambda i, at: (0, 0, 0))] * 4,
        ),
        out_shape=[jax.ShapeDtypeStruct((4, rows, width), jnp.bfloat16)] * 4,
        cost_estimate=BRIEF,
        name="adam_flips",
    )(at, *arrays)


def whole(kernel, out_shape, name, scalars, *arrays):
    vmem = pl.BlockSpec(memory_space=pltpu.VMEM)
    return pl.pallas_call(
        kernel,
        in_specs=[pl.BlockSpec(memory_space=pltpu.SMEM)] * len(scalars) + [vmem] * len(arrays),
        out_specs=jax.tree.map(lambda _: vmem, out_shape),
        out_shape=out_shape,
        compiler_params=pltpu.CompilerParams(vmem_limit_bytes=20 * 2**20),
        cost_estimate=BRIEF,
        name=name,
    )(*scalars, *arrays)


def regroup_kernel(*refs):
    for outer in range(4):
        for inner in range(4):
            refs[4 + inner][outer] = refs[outer][inner]


def regroup(parts):
    out = [jax.ShapeDtypeStruct(parts[0].shape, parts[0].dtype)] * 4
    return whole(regroup_kernel, out, "regroup", (), *parts)


def assemble_kernel(at_ref, *refs):
    out_ref = refs[4]
    rows = refs[0].shape[1]
    for z_flip in range(4):
        for y_flip in range(4):
            source = at_ref[y_flip] * 4 + (at_ref[4] ^ z_flip)
            place = pl.ds(pl.multiple_of(source * rows, rows), rows)
            out_ref[place] = refs[z_flip][y_flip]


def assemble(at, parts):
    out = jax.ShapeDtypeStruct((16 * parts[0].shape[1], parts[0].shape[2]), parts[0].dtype)
    return whole(assemble_kernel, out, "assemble", (at,), *parts)


def swap_axes_kernel(*refs):
    for flip in range(4):
        for flip_z in range(2):
            refs[4 + flip_z][flip] = refs[flip][flip_z]


def swap_axes(parts):
    out = [jax.ShapeDtypeStruct((4, *parts[0].shape[1:]), parts[0].dtype)] * 2
    return whole(swap_axes_kernel, out, "swap", (), *parts)


def interleave_kernel(first_ref, second_ref, out_ref):
    for flip in range(4):
        out_ref[2 * flip] = first_ref[flip]
        out_ref[2 * flip + 1] = second_ref[flip]


def interleave(first, second):
    out = jax.ShapeDtypeStruct((8, *first.shape[1:]), first.dtype)
    return whole(interleave_kernel, out, "interleave", (), first, second)


def column_kernel(*refs):
    for at in range(refs[-1].shape[0]):
        rows = [ref[at].astype(jnp.float32) for ref in refs[:-1]]
        refs[-1][at] = jnp.concatenate(rows, axis=0).astype(jnp.bfloat16)


def join_rows(parts):
    blocks, rows, width = parts[0].shape
    out = jax.ShapeDtypeStruct((blocks, len(parts) * rows, width), parts[0].dtype)
    return whole(column_kernel, out, "column", (), *parts)


def attend_kernel(
    to_ref, lengths_ref, query_ref, input_ref, new_k_ref, new_v_ref, old_k_ref, old_v_ref,
    gain_ref, *refs,
):
    *out_refs, summed_ref, normed_ref = refs
    rows = STEPS * ROWS_HERE
    stacked = GROUP * rows

    def flat(ref):
        return ref[...].astype(jnp.float32).reshape(rows, ref.shape[2])

    queries, new_k, new_v = flat(query_ref), flat(new_k_ref), flat(new_v_ref)
    new_k, new_v = new_k.astype(jnp.bfloat16), new_v.astype(jnp.bfloat16)
    at = lax.broadcasted_iota(jnp.int32, (stacked, CTX), 0)
    position = lax.broadcasted_iota(jnp.int32, (stacked, CTX), 1)
    first_row = at % ROWS_HERE == 0
    visible = position < jnp.where(first_row, lengths_ref[0], lengths_ref[1])
    at_new = lax.broadcasted_iota(jnp.int32, (stacked, rows), 0)
    key_new = lax.broadcasted_iota(jnp.int32, (stacked, rows), 1)
    visible_new = (key_new % ROWS_HERE == at_new % ROWS_HERE) & (
        key_new // ROWS_HERE <= at_new // ROWS_HERE % STEPS
    )

    def scores(query, keys):
        found = lax.dot_general(
            query, keys, (((1,), (1,)), ((), ())), preferred_element_type=jnp.float32
        )
        return found * HD ** (-0.5)

    def weighted(probs, values):
        return jnp.dot(probs, values, preferred_element_type=jnp.float32)

    squares = jnp.zeros((rows, HD), jnp.float32)
    for group in range(KVH):
        cols = slice(group * HD, (group + 1) * HD)
        heads = [
            slice((group * GROUP + j) * HD, (group * GROUP + j + 1) * HD) for j in range(GROUP)
        ]
        query = jnp.concatenate([queries[:, head] for head in heads], axis=0).astype(jnp.bfloat16)
        old = jnp.where(
            first_row, scores(query, old_k_ref[0, :, cols]), scores(query, old_k_ref[1, :, cols])
        )
        old = jnp.where(visible, old, -1e30)
        new = jnp.where(visible_new, scores(query, new_k[:, cols]), -1e30)
        peak = jnp.maximum(
            jnp.max(old, axis=1, keepdims=True), jnp.max(new, axis=1, keepdims=True)
        )
        old, new = jnp.exp(old - peak), jnp.exp(new - peak)
        total = jnp.sum(old, axis=1, keepdims=True) + jnp.sum(new, axis=1, keepdims=True)
        old, new = old / total, new / total
        attended = weighted(
            jnp.where(first_row, old, 0.0).astype(jnp.bfloat16), old_v_ref[0, :, cols]
        )
        attended += weighted(
            jnp.where(first_row, 0.0, old).astype(jnp.bfloat16), old_v_ref[1, :, cols]
        )
        attended += weighted(new.astype(jnp.bfloat16), new_v[:, cols])
        for j, head in enumerate(heads):
            part = input_ref[:, :, head].astype(jnp.float32).reshape(rows, HD)
            part += attended[j * rows : (j + 1) * rows]
            summed_ref[:, head] = part
            squares += part * part
    factor = lax.rsqrt(jnp.sum(squares, axis=1, keepdims=True) / D + 1e-06)
    for block in range(8):
        cols = slice(block * 1024, (block + 1) * 1024)
        gain = gain_ref[:, cols].astype(jnp.float32)
        normed_ref[block] = summed_ref[:, cols] * factor * gain
    mine = pl.ds(pl.multiple_of(to_ref[8] * 512, 512), 512)
    its = pl.ds(pl.multiple_of((1 - to_ref[8]) * 512, 512), 512)
    for flip, out_ref in enumerate(out_refs):
        for flip_z in range(2):
            chip = to_ref[2 * flip + flip_z]
            out_ref[flip_z, :, :512] = normed_ref[chip, :, mine].astype(jnp.bfloat16)
            out_ref[flip_z, :, 512:] = normed_ref[chip, :, its].astype(jnp.bfloat16)


def attend(to, lengths, *arrays):
    rows = STEPS * ROWS_HERE
    smem, vmem = pl.BlockSpec(memory_space=pltpu.SMEM), pl.BlockSpec(memory_space=pltpu.VMEM)
    return pl.pallas_call(
        attend_kernel,
        in_specs=[smem] * 2 + [vmem] * len(arrays),
        out_specs=[vmem] * 4,
        out_shape=[jax.ShapeDtypeStruct((2, rows, 1024), jnp.bfloat16)] * 4,
        scratch_shapes=[
            pltpu.VMEM((rows, D), jnp.float32),
            pltpu.VMEM((8, rows, 1024), jnp.float32),
        ],
        compiler_params=pltpu.CompilerParams(vmem_limit_bytes=12 * 2**20),
        cost_estimate=BRIEF,
        name="attend",
    )(to, lengths, *arrays)


def product_kernel(*refs):
    near_refs, far_refs = refs[:3], refs[3:5]
    own_ref, *piece_refs = refs[5:-6]
    send_a, keep_a, send_b, keep_b, new_ref, other_ref = refs[-6:]
    at = 0
    for ref in piece_refs:
        other_ref[at : at + ref.shape[0]] = ref[...]
        at += ref.shape[0]
    new_ref[...] = own_ref[...]
    half = own_ref.shape[1] // 2
    depth = own_ref.shape[0]
    for flip in (3, 1, 2, 0):
        parts = []
        for at in (2 * flip, 2 * flip + 1):
            parts += [ref[at] for ref in near_refs] + [far_refs[at // 4][at % 4]]
        rows = jnp.concatenate(parts, axis=0)
        total = jnp.dot(rows[:, :depth], own_ref[...], preferred_element_type=jnp.float32)
        total += jnp.dot(rows[:, depth:], other_ref[...], preferred_element_type=jnp.float32)
        term = (total * D ** (-0.5)).astype(jnp.bfloat16).reshape(2, 128, 2 * half)
        (send_a if flip & 1 else keep_a)[flip >> 1] = term[:, :, :half]
        (send_b if flip & 2 else keep_b)[flip & 1] = term[:, :, half:]


def products(row_parts, own, pieces, after=()):
    half = own.shape[1] // 2
    out = jax.ShapeDtypeStruct((2, 2, 128, half), jnp.bfloat16)
    vmem = pl.BlockSpec(memory_space=pltpu.VMEM)
    arrays = (*row_parts, own, *pieces)
    return pl.pallas_call(
        lambda *refs: product_kernel(*refs[: len(arrays)], *refs[-6:]),
        in_specs=[vmem] * len(arrays) + [pl.BlockSpec(memory_space=pl.ANY)] * len(after),
        out_specs=[vmem] * 5,
        out_shape=[out] * 4 + [jax.ShapeDtypeStruct(own.shape, own.dtype)],
        scratch_shapes=[pltpu.VMEM(own.shape, own.dtype)],
        compiler_params=pltpu.CompilerParams(vmem_limit_bytes=20 * 2**20),
        cost_estimate=BRIEF,
        name="products",
    )(*arrays, *after)


def add(kept, arrived):
    return kept.astype(jnp.float32) + arrived.astype(jnp.float32)


def over_z(parts):
    return [parts[0]] + [lax.ppermute(parts[k], "mp", mp_swap(0, k)) for k in (1, 2, 3)]


def over_y(parts):
    return [parts[0]] + [lax.ppermute(parts[k], "mp", mp_swap(k, 0)) for k in (1, 2, 3)]


def over_y_ring(column):
    near = [lax.ppermute(column, "mp", mp_swap(k, 0)) for k in (1, 2)]
    far = [
        lax.ppermute(near[0][:4], "mp", mp_swap(2, 0)),
        lax.ppermute(near[1][4:], "mp", mp_swap(1, 0)),
    ]
    return [column, *near, *far]


def swap_core(own, cuts):
    return [
        lax.ppermute(piece, "dp", dp_swap(0, 0, 1)) for piece in jnp.split(own, cuts)
    ]


def first_sums(parts):
    send_a, keep_a, send_b, keep_b = parts
    got_a = lax.ppermute(send_a, "dp", dp_swap(1, 0, 0))
    got_b = lax.ppermute(send_b, "dp", dp_swap(2, 0, 0))
    sends = [add(k[1], g[1]).astype(jnp.bfloat16) for k, g in ((keep_a, got_a), (keep_b, got_b))]
    return sends, [add(keep_a[0], got_a[0]), add(keep_b[0], got_b[0])]


def second_sums(sends, keeps):
    got_a = lax.ppermute(sends[0], "dp", dp_swap(2, 0, 0))
    got_b = lax.ppermute(sends[1], "dp", dp_swap(1, 0, 0))
    return jnp.concatenate([add(keeps[0], got_a), add(keeps[1], got_b)], axis=-1)


def last_sum(both):
    return add(both[0], lax.ppermute(both[1].astype(jnp.bfloat16), "dp", dp_swap(0, 1, 0)))


def local(
    weight_gate,
    weight_up,
    grad_gate,
    grad_up,
    moment_gate,
    moment_up,
    second_gate,
    second_up,
    layer_input,
    queries,
    fresh_keys,
    fresh_values,
    cached_keys,
    cached_values,
    lengths,
    norm_gain,
):
    dp = lax.axis_index("dp")
    mp = lax.axis_index("mp")
    x, z_hi, core = dp // 4, dp // 2 % 2, dp % 2
    y, z_lo = mp // 4, mp % 4
    gray_x, gray_y = x ^ (x >> 1), y ^ (y >> 1)

    def place(gray):
        return gray ^ (gray >> 1)

    at = jnp.stack([place(gray_y ^ flip) for flip in range(4)] + [z_lo]).astype(jnp.int32)
    to = jnp.stack(
        [place(gray_x ^ flip) * 2 + (z_hi ^ flip_z) for flip in range(4) for flip_z in range(2)]
        + [core]
    ).astype(jnp.int32)

    gate_step = adam_places(weight_gate, grad_gate, moment_gate, second_gate)
    gate_step, queries = lax.optimization_barrier((gate_step, queries))
    gate_own = lax.all_to_all(gate_step, "mp", split_axis=0, concat_axis=0, tiled=True)
    gate_own = gate_own.reshape(512, 1024)

    by_x = attend(
        to, lengths, queries, layer_input, fresh_keys, fresh_values, cached_keys, cached_values,
        norm_gain.reshape(1, D),
    )
    by_x, weight_up = lax.optimization_barrier((by_x, weight_up))
    up_parts = adam_flips(at, weight_up, grad_up, moment_up, second_up)
    by_x, up_parts = lax.optimization_barrier((by_x, up_parts))
    up_parts = over_y(up_parts)
    by_x = [by_x[0]] + [lax.ppermute(by_x[k], "dp", dp_swap(k, 0, 0)) for k in (1, 2, 3)]
    here, there = swap_axes(by_x)
    spread = interleave(here, lax.ppermute(there, "dp", dp_swap(0, 1, 0)))
    along_z = over_z([spread] * 4)
    column, up_parts, gate_own = lax.optimization_barrier(
        (join_rows(along_z), up_parts, gate_own)
    )
    gate_other = swap_core(gate_own, (176, 352))
    row_parts = over_y_ring(column)
    up_parts = over_z(regroup(up_parts))
    *gate_terms, gate_new = products(row_parts, gate_own, gate_other, up_parts[1:3])
    gate_new, up_parts = lax.optimization_barrier((gate_new, up_parts))
    up_own = assemble(at, up_parts)
    *up_terms, up_new = products(row_parts, up_own, swap_core(up_own, (256,)))

    gate_terms[1], gate_terms[3], up_new = lax.optimization_barrier(
        (gate_terms[1], gate_terms[3], up_new)
    )
    gate_sends, gate_keeps = first_sums(gate_terms)
    gate_sends, up_terms = lax.optimization_barrier((gate_sends, up_terms))
    gate_both = second_sums(gate_sends, gate_keeps)
    up_both = second_sums(*first_sums(up_terms))
    gate_total, up_both = lax.optimization_barrier((last_sum(gate_both), up_both))
    up_total = last_sum(up_both)
    hidden = (jax.nn.silu(gate_total) * up_total).astype(jnp.bfloat16)

    row = jnp.arange(128)
    y_flip, z_flip, step_at, row_at = row // 32, row // 8 % 4, row // 2 % 4, row % 2
    target = step_at * 32 + (place(gray_y ^ y_flip) * 4 + (z_lo ^ z_flip)) * 2 + row_at
    placed = (row[:, None] == target[None, :]).astype(jnp.bfloat16)
    hidden = jnp.dot(placed, hidden, preferred_element_type=jnp.float32).astype(jnp.bfloat16)
    return gate_new, up_new, hidden.reshape(STEPS, 32, 1024)


def solution(mesh):
    rows = P(("dp", "mp"), None)
    steps = P(None, ("dp", "mp"), None)
    cache = P(("dp", "mp"), None, None)
    in_specs = (rows,) * 8 + (steps,) * 4 + (cache,) * 2 + (P(("dp", "mp")), P())
    out_specs = (P("dp", "mp"), P("dp", "mp"), P(None, "dp", "mp"))
    return jax.shard_map(local, mesh=mesh, in_specs=in_specs, out_specs=out_specs, check_vma=False)
```

```python
import jax
import jax.numpy as jnp
from jax import lax
from jax.experimental import pallas as pl
from jax.experimental.pallas import tpu as pltpu
from jax.sharding import PartitionSpec as P

D = 8192
HD = 128
KVH = 8
GROUP = 8
CTX = 128
STEPS = 4
ROWS_HERE = 2

PIECE = 256
BRIEF = pl.CostEstimate(flops=1, bytes_accessed=1, transcendentals=0)

GRAY = (0, 1, 3, 2)

beta_one = 0.9
beta_two = 0.95
learn_rate = 0.15
weight_decay = 0.1
adam_eps = 1e-08
first_fix = 1.0 - 0.9**10
second_fix = 1.0 - 0.95**10


def dp_swap(flip_x, flip_z, flip_core):
    pairs = []
    for dp in range(16):
        x, z_hi, core = dp // 4, dp // 2 % 2, dp % 2
        x_to = GRAY[GRAY[x] ^ flip_x]
        pairs.append((dp, x_to * 4 + (z_hi ^ flip_z) * 2 + (core ^ flip_core)))
    return pairs


def mp_swap(flip_y, flip_z):
    pairs = []
    for mp in range(16):
        y, z_lo = mp // 4, mp % 4
        pairs.append((mp, GRAY[GRAY[y] ^ flip_y] * 4 + (z_lo ^ flip_z)))
    return pairs


def adam_kernel(weight_ref, grad_ref, moment_ref, second_ref, cols):
    weight_f = weight_ref[:, cols].astype(jnp.float32)
    grad_f = grad_ref[:, cols].astype(jnp.float32)
    moment_f = moment_ref[:, cols].astype(jnp.float32)
    second_f = second_ref[:, cols].astype(jnp.float32)
    rise = (learn_rate * beta_one / first_fix) * moment_f
    rise += (learn_rate * (1.0 - beta_one) / first_fix) * grad_f
    spread = (beta_two / second_fix) * second_f
    spread += ((1.0 - beta_two) / second_fix) * (grad_f * grad_f)
    root = spread * lax.rsqrt(spread) + adam_eps
    new = (1.0 - learn_rate * weight_decay) * weight_f - rise * lax.rsqrt(root * root)
    return new.astype(jnp.bfloat16)


def adam_places_kernel(*refs):
    *in_refs, out_ref = refs
    parts, _, width = out_ref.shape
    for part in range(parts):
        for at in range(0, width, PIECE):
            cols = pl.ds(part * width + at, PIECE)
            out_ref[part, :, at : at + PIECE] = adam_kernel(*in_refs, cols)


def adam_places(*arrays):
    rows, cols = arrays[0].shape
    width = cols // 16
    return pl.pallas_call(
        adam_places_kernel,
        grid=(2,),
        in_specs=[pl.BlockSpec((rows, 8 * width), lambda i: (0, i))] * 4,
        out_specs=pl.BlockSpec((8, rows, width), lambda i: (i, 0, 0)),
        out_shape=jax.ShapeDtypeStruct((16, rows, width), jnp.bfloat16),
        cost_estimate=BRIEF,
        name="adam_places",
    )(*arrays)


def adam_flips_kernel(to_ref, *refs):
    in_refs, out_refs = refs[:8], refs[8:]
    width = out_refs[0].shape[2]
    for half in range(2):
        for flip in range(4):
            cols = pl.ds(pl.multiple_of((to_ref[13] ^ flip) * width, width), width)
            new = adam_kernel(*in_refs[half::2], cols)
            for step in range(2):

                @pl.when(pl.program_id(0) == step)
                def _():
                    out_refs[2 * step + half][flip] = new


def adam_flips(to, *arrays):
    rows, cols = arrays[0].shape
    width = cols // 16
    in_specs = [
        pl.BlockSpec((rows, 4 * width), lambda i, to: (0, to[9 + 2 * i])),
        pl.BlockSpec((rows, 4 * width), lambda i, to: (0, to[10 + 2 * i])),
    ]
    return pl.pallas_call(
        adam_flips_kernel,
        grid_spec=pltpu.PrefetchScalarGridSpec(
            num_scalar_prefetch=1,
            grid=(2,),
            in_specs=in_specs * 4,
            out_specs=[pl.BlockSpec((4, rows, width), lambda i, to: (0, 0, 0))] * 4,
        ),
        out_shape=[jax.ShapeDtypeStruct((4, rows, width), jnp.bfloat16)] * 4,
        cost_estimate=BRIEF,
        name="adam_flips",
    )(to, *[array for array in arrays for _ in range(2)])


def whole(kernel, out_shape, name, scalars, *arrays):
    vmem = pl.BlockSpec(memory_space=pltpu.VMEM)
    return pl.pallas_call(
        kernel,
        in_specs=[pl.BlockSpec(memory_space=pltpu.SMEM)] * len(scalars) + [vmem] * len(arrays),
        out_specs=jax.tree.map(lambda _: vmem, out_shape),
        out_shape=out_shape,
        compiler_params=pltpu.CompilerParams(vmem_limit_bytes=20 * 2**20),
        cost_estimate=BRIEF,
        name=name,
    )(*scalars, *arrays)


def regroup_kernel(*refs):
    for outer in range(4):
        for inner in range(4):
            refs[4 + inner][outer] = refs[outer][inner]


def regroup(parts):
    out = [jax.ShapeDtypeStruct(parts[0].shape, parts[0].dtype)] * 4
    return whole(regroup_kernel, out, "regroup", (), *parts)


def assemble_into(out_ref, to_ref, *refs):
    rows = refs[0].shape[1]
    for z_flip in range(4):
        for y_flip in range(4):
            source = to_ref[9 + y_flip] * 4 + (to_ref[13] ^ z_flip)
            place = pl.ds(pl.multiple_of(source * rows, rows), rows)
            out_ref[place] = refs[z_flip][y_flip]


def swap_axes_kernel(*refs):
    for flip in range(4):
        for flip_z in range(2):
            refs[4 + flip_z][flip] = refs[flip][flip_z]


def swap_axes(parts):
    out = [jax.ShapeDtypeStruct((4, *parts[0].shape[1:]), parts[0].dtype)] * 2
    return whole(swap_axes_kernel, out, "swap", (), *parts)


def interleave_kernel(first_ref, second_ref, out_ref):
    for flip in range(4):
        out_ref[2 * flip] = first_ref[flip]
        out_ref[2 * flip + 1] = second_ref[flip]


def interleave(first, second):
    out = jax.ShapeDtypeStruct((8, *first.shape[1:]), first.dtype)
    return whole(interleave_kernel, out, "interleave", (), first, second)


def column_kernel(*refs):
    for at in range(refs[-1].shape[0]):
        rows = [ref[at].astype(jnp.float32) for ref in refs[:-1]]
        refs[-1][at] = jnp.concatenate(rows, axis=0).astype(jnp.bfloat16)


def join_rows(parts):
    blocks, rows, width = parts[0].shape
    out = jax.ShapeDtypeStruct((blocks, len(parts) * rows, width), parts[0].dtype)
    return whole(column_kernel, out, "column", (), *parts)


def attend_kernel(
    to_ref, lengths_ref, query_ref, input_ref, new_k_ref, new_v_ref, old_k_ref, old_v_ref,
    gain_ref, *refs,
):
    *out_refs, summed_ref, normed_ref = refs
    rows = STEPS * ROWS_HERE
    stacked = GROUP * rows

    def flat(ref):
        return ref[...].astype(jnp.float32).reshape(rows, ref.shape[2])

    queries, new_k, new_v = flat(query_ref), flat(new_k_ref), flat(new_v_ref)
    new_k, new_v = new_k.astype(jnp.bfloat16), new_v.astype(jnp.bfloat16)
    at = lax.broadcasted_iota(jnp.int32, (stacked, CTX), 0)
    position = lax.broadcasted_iota(jnp.int32, (stacked, CTX), 1)
    first_row = at % ROWS_HERE == 0
    visible = position < jnp.where(first_row, lengths_ref[0], lengths_ref[1])
    at_new = lax.broadcasted_iota(jnp.int32, (stacked, rows), 0)
    key_new = lax.broadcasted_iota(jnp.int32, (stacked, rows), 1)
    visible_new = (key_new % ROWS_HERE == at_new % ROWS_HERE) & (
        key_new // ROWS_HERE <= at_new // ROWS_HERE % STEPS
    )

    def scores(query, keys):
        found = lax.dot_general(
            query, keys, (((1,), (1,)), ((), ())), preferred_element_type=jnp.float32
        )
        return found * HD ** (-0.5)

    def weighted(probs, values):
        return jnp.dot(probs, values, preferred_element_type=jnp.float32)

    squares = jnp.zeros((rows, HD), jnp.float32)
    for group in range(KVH):
        cols = slice(group * HD, (group + 1) * HD)
        heads = [
            slice((group * GROUP + j) * HD, (group * GROUP + j + 1) * HD) for j in range(GROUP)
        ]
        query = jnp.concatenate([queries[:, head] for head in heads], axis=0).astype(jnp.bfloat16)
        old = jnp.where(
            first_row, scores(query, old_k_ref[0, :, cols]), scores(query, old_k_ref[1, :, cols])
        )
        old = jnp.where(visible, old, -1e30)
        new = jnp.where(visible_new, scores(query, new_k[:, cols]), -1e30)
        peak = jnp.maximum(
            jnp.max(old, axis=1, keepdims=True), jnp.max(new, axis=1, keepdims=True)
        )
        old, new = jnp.exp(old - peak), jnp.exp(new - peak)
        total = jnp.sum(old, axis=1, keepdims=True) + jnp.sum(new, axis=1, keepdims=True)
        old, new = old / total, new / total
        attended = weighted(
            jnp.where(first_row, old, 0.0).astype(jnp.bfloat16), old_v_ref[0, :, cols]
        )
        attended += weighted(
            jnp.where(first_row, 0.0, old).astype(jnp.bfloat16), old_v_ref[1, :, cols]
        )
        attended += weighted(new.astype(jnp.bfloat16), new_v[:, cols])
        for j, head in enumerate(heads):
            part = input_ref[:, :, head].astype(jnp.float32).reshape(rows, HD)
            part += attended[j * rows : (j + 1) * rows]
            summed_ref[:, head] = part
            squares += part * part
    factor = lax.rsqrt(jnp.sum(squares, axis=1, keepdims=True) / D + 1e-06)
    for block in range(8):
        cols = slice(block * 1024, (block + 1) * 1024)
        gain = gain_ref[:, cols].astype(jnp.float32)
        normed_ref[block] = summed_ref[:, cols] * factor * gain
    mine = pl.ds(pl.multiple_of(to_ref[8] * 512, 512), 512)
    its = pl.ds(pl.multiple_of((1 - to_ref[8]) * 512, 512), 512)
    for flip, out_ref in enumerate(out_refs):
        for flip_z in range(2):
            chip = to_ref[2 * flip + flip_z]
            out_ref[flip_z, :, :512] = normed_ref[chip, :, mine].astype(jnp.bfloat16)
            out_ref[flip_z, :, 512:] = normed_ref[chip, :, its].astype(jnp.bfloat16)


def attend(to, lengths, *arrays):
    rows = STEPS * ROWS_HERE
    smem, vmem = pl.BlockSpec(memory_space=pltpu.SMEM), pl.BlockSpec(memory_space=pltpu.VMEM)
    return pl.pallas_call(
        attend_kernel,
        in_specs=[smem] * 2 + [vmem] * len(arrays),
        out_specs=[vmem] * 4,
        out_shape=[jax.ShapeDtypeStruct((2, rows, 1024), jnp.bfloat16)] * 4,
        scratch_shapes=[
            pltpu.VMEM((rows, D), jnp.float32),
            pltpu.VMEM((8, rows, 1024), jnp.float32),
        ],
        compiler_params=pltpu.CompilerParams(vmem_limit_bytes=12 * 2**20),
        cost_estimate=BRIEF,
        name="attend",
    )(to, lengths, *arrays)


def product_kernel(row_refs, own_ref, other_ref, send_a, keep_a, send_b, keep_b):
    near_refs, far_refs = row_refs[:3], row_refs[3:]
    half = own_ref.shape[1] // 2
    depth = own_ref.shape[0]
    for flip in (3, 1, 2, 0):
        parts = []
        for at in (2 * flip, 2 * flip + 1):
            parts += [ref[at] for ref in near_refs] + [far_refs[at // 4][at % 4]]
        rows = jnp.concatenate(parts, axis=0)
        total = jnp.dot(rows[:, :depth], own_ref[...], preferred_element_type=jnp.float32)
        total += jnp.dot(rows[:, depth:], other_ref[...], preferred_element_type=jnp.float32)
        term = (total * D ** (-0.5)).astype(jnp.bfloat16).reshape(2, 128, 2 * half)
        (send_a if flip & 1 else keep_a)[flip >> 1] = term[:, :, :half]
        (send_b if flip & 2 else keep_b)[flip & 1] = term[:, :, half:]


def first_kernel(*refs):
    row_refs, own_ref, piece_refs = refs[:5], refs[5], refs[6:10]
    *term_refs, new_ref, other_ref = refs[-6:]
    new_ref[...] = own_ref[...]
    at = 0
    for ref in piece_refs:
        other_ref[at : at + ref.shape[0]] = ref[...]
        at += ref.shape[0]
    product_kernel(row_refs, own_ref, other_ref, *term_refs)


def second_kernel(to_ref, *refs):
    *term_refs, new_ref, other_ref = refs[-6:]
    assemble_into(new_ref, to_ref, *refs[5:9])
    assemble_into(other_ref, to_ref, *refs[9:13])
    product_kernel(refs[:5], new_ref, other_ref, *term_refs)


def products(kernel, scalars, row_parts, weights, after=()):
    term = jax.ShapeDtypeStruct((2, 2, 128, 512), jnp.bfloat16)
    own = jax.ShapeDtypeStruct((512, 1024), jnp.bfloat16)
    vmem = pl.BlockSpec(memory_space=pltpu.VMEM)
    arrays = (*scalars, *row_parts, *weights)
    return pl.pallas_call(
        lambda *refs: kernel(*refs[: len(arrays)], *refs[-6:]),
        in_specs=[pl.BlockSpec(memory_space=pltpu.SMEM)] * len(scalars)
        + [vmem] * (len(arrays) - len(scalars))
        + [pl.BlockSpec(memory_space=pl.ANY)] * len(after),
        out_specs=[vmem] * 5,
        out_shape=[term] * 4 + [own],
        scratch_shapes=[pltpu.VMEM(own.shape, own.dtype)],
        compiler_params=pltpu.CompilerParams(vmem_limit_bytes=20 * 2**20),
        cost_estimate=BRIEF,
        name="products",
    )(*arrays, *after)


def add(kept, arrived):
    return kept.astype(jnp.float32) + arrived.astype(jnp.float32)


def over_z(parts):
    return [parts[0]] + [lax.ppermute(parts[k], "mp", mp_swap(0, k)) for k in (1, 2, 3)]


def over_y(parts):
    return [parts[0]] + [lax.ppermute(parts[k], "mp", mp_swap(k, 0)) for k in (1, 2, 3)]


def over_y_ring(column):
    near = [lax.ppermute(column, "mp", mp_swap(k, 0)) for k in (1, 2)]
    far = [
        lax.ppermute(near[0][:4], "mp", mp_swap(2, 0)),
        lax.ppermute(near[1][4:], "mp", mp_swap(1, 0)),
    ]
    return [column, *near, *far]


def swap_core(own, cuts):
    return [
        lax.ppermute(piece, "dp", dp_swap(0, 0, 1)) for piece in jnp.split(own, cuts)
    ]


def first_sums(parts):
    send_a, keep_a, send_b, keep_b = parts
    got_a = lax.ppermute(send_a, "dp", dp_swap(1, 0, 0))
    got_b = lax.ppermute(send_b, "dp", dp_swap(2, 0, 0))
    sends = [add(k[1], g[1]).astype(jnp.bfloat16) for k, g in ((keep_a, got_a), (keep_b, got_b))]
    return sends, [add(keep_a[0], got_a[0]), add(keep_b[0], got_b[0])]


def second_sums(sends, keeps):
    got_a = lax.ppermute(sends[0], "dp", dp_swap(2, 0, 0))
    got_b = lax.ppermute(sends[1], "dp", dp_swap(1, 0, 0))
    return jnp.concatenate([add(keeps[0], got_a), add(keeps[1], got_b)], axis=-1)


def last_sum(both):
    return add(both[0], lax.ppermute(both[1].astype(jnp.bfloat16), "dp", dp_swap(0, 1, 0)))


def local(
    weight_gate,
    weight_up,
    grad_gate,
    grad_up,
    moment_gate,
    moment_up,
    second_gate,
    second_up,
    layer_input,
    queries,
    fresh_keys,
    fresh_values,
    cached_keys,
    cached_values,
    lengths,
    norm_gain,
):
    dp = lax.axis_index("dp")
    mp = lax.axis_index("mp")
    x, z_hi, core = dp // 4, dp // 2 % 2, dp % 2
    y, z_lo = mp // 4, mp % 4
    gray_x, gray_y = x ^ (x >> 1), y ^ (y >> 1)

    def place(gray):
        return gray ^ (gray >> 1)

    to = jnp.stack(
        [place(gray_x ^ flip) * 2 + (z_hi ^ flip_z) for flip in range(4) for flip_z in range(2)]
        + [core]
        + [place(gray_y ^ flip) for flip in range(4)]
        + [z_lo]
    ).astype(jnp.int32)

    gate_step = adam_places(weight_gate, grad_gate, moment_gate, second_gate)
    gate_step, lengths = lax.optimization_barrier((gate_step, lengths))
    gate_own = lax.all_to_all(gate_step, "mp", split_axis=0, concat_axis=0, tiled=True)
    gate_own = gate_own.reshape(512, 1024)

    by_x = attend(
        to, lengths, queries, layer_input, fresh_keys, fresh_values, cached_keys, cached_values,
        norm_gain.reshape(1, D),
    )
    by_x, weight_up = lax.optimization_barrier((by_x, weight_up))
    up_parts = adam_flips(to, weight_up, grad_up, moment_up, second_up)
    by_x, up_parts = lax.optimization_barrier((by_x, up_parts))
    up_parts = over_y(up_parts)
    by_x = [by_x[0]] + [lax.ppermute(by_x[k], "dp", dp_swap(k, 0, 0)) for k in (1, 2, 3)]
    here, there = swap_axes(by_x)
    spread = interleave(here, lax.ppermute(there, "dp", dp_swap(0, 1, 0)))
    along_z = over_z([spread] * 4)
    column, up_parts, gate_own = lax.optimization_barrier(
        (join_rows(along_z), up_parts, gate_own)
    )
    gate_other = swap_core(gate_own, (128, 256, 384))
    row_parts = over_y_ring(column)
    up_parts = over_z(regroup(up_parts))
    *gate_terms, gate_new = products(
        first_kernel, (), row_parts, (gate_own, *gate_other), up_parts[1:3]
    )
    gate_new, up_parts[3] = lax.optimization_barrier((gate_new, up_parts[3]))
    up_other = [swap_core(part, ())[0] for part in up_parts]
    *up_terms, up_new = products(second_kernel, (to,), row_parts, (*up_parts, *up_other))

    gate_terms[1], gate_terms[3], up_new = lax.optimization_barrier(
        (gate_terms[1], gate_terms[3], up_new)
    )
    gate_sends, gate_keeps = first_sums(gate_terms)
    gate_sends, up_terms = lax.optimization_barrier((gate_sends, up_terms))
    gate_both = second_sums(gate_sends, gate_keeps)
    up_both = second_sums(*first_sums(up_terms))
    gate_total, up_both = lax.optimization_barrier((last_sum(gate_both), up_both))
    up_total = last_sum(up_both)
    hidden = (jax.nn.silu(gate_total) * up_total).astype(jnp.bfloat16)

    row = jnp.arange(128)
    y_flip, z_flip, step_at, row_at = row // 32, row // 8 % 4, row // 2 % 4, row % 2
    target = step_at * 32 + (place(gray_y ^ y_flip) * 4 + (z_lo ^ z_flip)) * 2 + row_at
    placed = (row[:, None] == target[None, :]).astype(jnp.bfloat16)
    hidden = jnp.dot(placed, hidden, preferred_element_type=jnp.float32).astype(jnp.bfloat16)
    return gate_new, up_new, hidden.reshape(STEPS, 32, 1024)


def solution(mesh):
    rows = P(("dp", "mp"), None)
    steps = P(None, ("dp", "mp"), None)
    cache = P(("dp", "mp"), None, None)
    in_specs = (rows,) * 8 + (steps,) * 4 + (cache,) * 2 + (P(("dp", "mp")), P())
    out_specs = (P("dp", "mp"), P("dp", "mp"), P(None, "dp", "mp"))
    return jax.shard_map(local, mesh=mesh, in_specs=in_specs, out_specs=out_specs, check_vma=False)
```

```python
import jax
import jax.numpy as jnp
from jax import lax
from jax.experimental import pallas as pl
from jax.experimental.pallas import tpu as pltpu
from jax.sharding import PartitionSpec as P

D = 8192
HD = 128
KVH = 8
GROUP = 8
CTX = 128
STEPS = 4
ROWS_HERE = 2

PIECE = 256
BRIEF = pl.CostEstimate(flops=1, bytes_accessed=1, transcendentals=0)

GRAY = (0, 1, 3, 2)

beta_one = 0.9
beta_two = 0.95
learn_rate = 0.15
weight_decay = 0.1
adam_eps = 1e-08
first_fix = 1.0 - 0.9**10
second_fix = 1.0 - 0.95**10


def dp_swap(flip_x, flip_z, flip_core):
    pairs = []
    for dp in range(16):
        x, z_hi, core = dp // 4, dp // 2 % 2, dp % 2
        x_to = GRAY[GRAY[x] ^ flip_x]
        pairs.append((dp, x_to * 4 + (z_hi ^ flip_z) * 2 + (core ^ flip_core)))
    return pairs


def mp_swap(flip_y, flip_z):
    pairs = []
    for mp in range(16):
        y, z_lo = mp // 4, mp % 4
        pairs.append((mp, GRAY[GRAY[y] ^ flip_y] * 4 + (z_lo ^ flip_z)))
    return pairs


def adam_kernel(weight_ref, grad_ref, moment_ref, second_ref, cols):
    weight_f = weight_ref[:, cols].astype(jnp.float32)
    grad_f = grad_ref[:, cols].astype(jnp.float32)
    moment_f = moment_ref[:, cols].astype(jnp.float32)
    second_f = second_ref[:, cols].astype(jnp.float32)
    rise = (learn_rate * beta_one / first_fix) * moment_f
    rise += (learn_rate * (1.0 - beta_one) / first_fix) * grad_f
    spread = (beta_two / second_fix) * second_f
    spread += ((1.0 - beta_two) / second_fix) * (grad_f * grad_f)
    root = spread * lax.rsqrt(spread) + adam_eps
    new = (1.0 - learn_rate * weight_decay) * weight_f - rise * lax.rsqrt(root * root)
    return new.astype(jnp.bfloat16)


def adam_places_kernel(*refs):
    *in_refs, out_ref = refs
    parts, _, width = out_ref.shape
    for part in range(parts):
        for at in range(0, width, PIECE):
            cols = pl.ds(part * width + at, PIECE)
            out_ref[part, :, at : at + PIECE] = adam_kernel(*in_refs, cols)


def adam_places(*arrays):
    rows, cols = arrays[0].shape
    width = cols // 16
    return pl.pallas_call(
        adam_places_kernel,
        grid=(2,),
        in_specs=[pl.BlockSpec((rows, 8 * width), lambda i: (0, i))] * 4,
        out_specs=pl.BlockSpec((8, rows, width), lambda i: (i, 0, 0)),
        out_shape=jax.ShapeDtypeStruct((16, rows, width), jnp.bfloat16),
        cost_estimate=BRIEF,
        name="adam_places",
    )(*arrays)


def adam_flips_kernel(to_ref, *refs):
    in_refs, out_refs = refs[:8], refs[8:]
    width = out_refs[0].shape[2]
    for half in range(2):
        for flip in range(4):
            cols = pl.ds(pl.multiple_of((to_ref[13] ^ flip) * width, width), width)
            new = adam_kernel(*in_refs[half::2], cols)
            for step in range(2):

                @pl.when(pl.program_id(0) == step)
                def _():
                    out_refs[2 * step + half][flip] = new


def adam_flips(to, *arrays):
    rows, cols = arrays[0].shape
    width = cols // 16
    in_specs = [
        pl.BlockSpec((rows, 4 * width), lambda i, to: (0, to[9 + 2 * i])),
        pl.BlockSpec((rows, 4 * width), lambda i, to: (0, to[10 + 2 * i])),
    ]
    return pl.pallas_call(
        adam_flips_kernel,
        grid_spec=pltpu.PrefetchScalarGridSpec(
            num_scalar_prefetch=1,
            grid=(2,),
            in_specs=in_specs * 4,
            out_specs=[pl.BlockSpec((4, rows, width), lambda i, to: (0, 0, 0))] * 4,
        ),
        out_shape=[jax.ShapeDtypeStruct((4, rows, width), jnp.bfloat16)] * 4,
        cost_estimate=BRIEF,
        name="adam_flips",
    )(to, *[array for array in arrays for _ in range(2)])


def whole(kernel, out_shape, name, scalars, *arrays):
    vmem = pl.BlockSpec(memory_space=pltpu.VMEM)
    return pl.pallas_call(
        kernel,
        in_specs=[pl.BlockSpec(memory_space=pltpu.SMEM)] * len(scalars) + [vmem] * len(arrays),
        out_specs=jax.tree.map(lambda _: vmem, out_shape),
        out_shape=out_shape,
        compiler_params=pltpu.CompilerParams(vmem_limit_bytes=20 * 2**20),
        cost_estimate=BRIEF,
        name=name,
    )(*scalars, *arrays)


def regroup_kernel(*refs):
    for outer in range(4):
        for inner in range(4):
            refs[4 + inner][outer] = refs[outer][inner]


def regroup(parts):
    out = [jax.ShapeDtypeStruct(parts[0].shape, parts[0].dtype)] * 4
    return whole(regroup_kernel, out, "regroup", (), *parts)


def assemble_into(out_ref, to_ref, *refs):
    rows = refs[0].shape[1]
    for z_flip in range(4):
        for y_flip in range(4):
            source = to_ref[9 + y_flip] * 4 + (to_ref[13] ^ z_flip)
            place = pl.ds(pl.multiple_of(source * rows, rows), rows)
            out_ref[place] = refs[z_flip][y_flip]


def swap_axes_kernel(*refs):
    for flip in range(4):
        for flip_z in range(2):
            refs[4 + flip_z][flip] = refs[flip][flip_z]


def swap_axes(parts):
    out = [jax.ShapeDtypeStruct((4, *parts[0].shape[1:]), parts[0].dtype)] * 2
    return whole(swap_axes_kernel, out, "swap", (), *parts)


def interleave_kernel(first_ref, second_ref, out_ref):
    for flip in range(4):
        out_ref[2 * flip] = first_ref[flip]
        out_ref[2 * flip + 1] = second_ref[flip]


def interleave(first, second):
    out = jax.ShapeDtypeStruct((8, *first.shape[1:]), first.dtype)
    return whole(interleave_kernel, out, "interleave", (), first, second)


def column_kernel(*refs):
    for at in range(refs[-1].shape[0]):
        rows = [ref[at].astype(jnp.float32) for ref in refs[:-1]]
        refs[-1][at] = jnp.concatenate(rows, axis=0).astype(jnp.bfloat16)


def join_rows(parts):
    blocks, rows, width = parts[0].shape
    out = jax.ShapeDtypeStruct((blocks, len(parts) * rows, width), parts[0].dtype)
    return whole(column_kernel, out, "column", (), *parts)


def attend_kernel(
    to_ref, lengths_ref, query_ref, input_ref, new_k_ref, new_v_ref, old_k_ref, old_v_ref,
    gain_ref, *refs,
):
    *out_refs, summed_ref, normed_ref = refs
    rows = STEPS * ROWS_HERE
    stacked = GROUP * rows

    def flat(ref):
        return ref[...].astype(jnp.float32).reshape(rows, ref.shape[2])

    queries, new_k, new_v = flat(query_ref), flat(new_k_ref), flat(new_v_ref)
    new_k, new_v = new_k.astype(jnp.bfloat16), new_v.astype(jnp.bfloat16)
    at = lax.broadcasted_iota(jnp.int32, (stacked, CTX), 0)
    position = lax.broadcasted_iota(jnp.int32, (stacked, CTX), 1)
    first_row = at % ROWS_HERE == 0
    visible = position < jnp.where(first_row, lengths_ref[0], lengths_ref[1])
    at_new = lax.broadcasted_iota(jnp.int32, (stacked, rows), 0)
    key_new = lax.broadcasted_iota(jnp.int32, (stacked, rows), 1)
    visible_new = (key_new % ROWS_HERE == at_new % ROWS_HERE) & (
        key_new // ROWS_HERE <= at_new // ROWS_HERE % STEPS
    )

    def scores(query, keys):
        found = lax.dot_general(
            query, keys, (((1,), (1,)), ((), ())), preferred_element_type=jnp.float32
        )
        return found * HD ** (-0.5)

    def weighted(probs, values):
        return jnp.dot(probs, values, preferred_element_type=jnp.float32)

    squares = jnp.zeros((rows, HD), jnp.float32)
    for group in range(KVH):
        cols = slice(group * HD, (group + 1) * HD)
        heads = [
            slice((group * GROUP + j) * HD, (group * GROUP + j + 1) * HD) for j in range(GROUP)
        ]
        query = jnp.concatenate([queries[:, head] for head in heads], axis=0).astype(jnp.bfloat16)
        old = jnp.where(
            first_row, scores(query, old_k_ref[0, :, cols]), scores(query, old_k_ref[1, :, cols])
        )
        old = jnp.where(visible, old, -1e30)
        new = jnp.where(visible_new, scores(query, new_k[:, cols]), -1e30)
        peak = jnp.maximum(
            jnp.max(old, axis=1, keepdims=True), jnp.max(new, axis=1, keepdims=True)
        )
        old, new = jnp.exp(old - peak), jnp.exp(new - peak)
        total = jnp.sum(old, axis=1, keepdims=True) + jnp.sum(new, axis=1, keepdims=True)
        old, new = old / total, new / total
        attended = weighted(
            jnp.where(first_row, old, 0.0).astype(jnp.bfloat16), old_v_ref[0, :, cols]
        )
        attended += weighted(
            jnp.where(first_row, 0.0, old).astype(jnp.bfloat16), old_v_ref[1, :, cols]
        )
        attended += weighted(new.astype(jnp.bfloat16), new_v[:, cols])
        for j, head in enumerate(heads):
            part = input_ref[:, :, head].astype(jnp.float32).reshape(rows, HD)
            part += attended[j * rows : (j + 1) * rows]
            summed_ref[:, head] = part
            squares += part * part
    factor = lax.rsqrt(jnp.sum(squares, axis=1, keepdims=True) / D + 1e-06)
    for block in range(8):
        cols = slice(block * 1024, (block + 1) * 1024)
        gain = gain_ref[:, cols].astype(jnp.float32)
        normed_ref[block] = summed_ref[:, cols] * factor * gain
    mine = pl.ds(pl.multiple_of(to_ref[8] * 512, 512), 512)
    its = pl.ds(pl.multiple_of((1 - to_ref[8]) * 512, 512), 512)
    for flip, out_ref in enumerate(out_refs):
        for flip_z in range(2):
            chip = to_ref[2 * flip + flip_z]
            out_ref[flip_z, :, :512] = normed_ref[chip, :, mine].astype(jnp.bfloat16)
            out_ref[flip_z, :, 512:] = normed_ref[chip, :, its].astype(jnp.bfloat16)


def attend(to, lengths, *arrays):
    rows = STEPS * ROWS_HERE
    smem, vmem = pl.BlockSpec(memory_space=pltpu.SMEM), pl.BlockSpec(memory_space=pltpu.VMEM)
    return pl.pallas_call(
        attend_kernel,
        in_specs=[smem] * 2 + [vmem] * len(arrays),
        out_specs=[vmem] * 4,
        out_shape=[jax.ShapeDtypeStruct((2, rows, 1024), jnp.bfloat16)] * 4,
        scratch_shapes=[
            pltpu.VMEM((rows, D), jnp.float32),
            pltpu.VMEM((8, rows, 1024), jnp.float32),
        ],
        compiler_params=pltpu.CompilerParams(vmem_limit_bytes=12 * 2**20),
        cost_estimate=BRIEF,
        name="attend",
    )(to, lengths, *arrays)


def product_kernel(row_refs, own_ref, other_ref, send_a, keep_a, send_b, keep_b):
    near_refs, far_refs = row_refs[:3], row_refs[3:]
    half = own_ref.shape[1] // 2
    depth = own_ref.shape[0]
    for flip in (3, 1, 2, 0):
        parts = []
        for at in (2 * flip, 2 * flip + 1):
            parts += [ref[at] for ref in near_refs] + [far_refs[at // 4][at % 4]]
        rows = jnp.concatenate(parts, axis=0)
        total = jnp.dot(rows[:, :depth], own_ref[...], preferred_element_type=jnp.float32)
        total += jnp.dot(rows[:, depth:], other_ref[...], preferred_element_type=jnp.float32)
        term = (total * D ** (-0.5)).astype(jnp.bfloat16).reshape(2, 128, 2 * half)
        (send_a if flip & 1 else keep_a)[flip >> 1] = term[:, :, :half]
        (send_b if flip & 2 else keep_b)[flip & 1] = term[:, :, half:]


def first_kernel(*refs):
    row_refs, own_ref, piece_refs = refs[:5], refs[5], refs[6:-6]
    *term_refs, new_ref, other_ref = refs[-6:]
    new_ref[...] = own_ref[...]
    at = 0
    for ref in piece_refs:
        other_ref[at : at + ref.shape[0]] = ref[...]
        at += ref.shape[0]
    product_kernel(row_refs, own_ref, other_ref, *term_refs)


def second_kernel(to_ref, *refs):
    *term_refs, new_ref, other_ref = refs[-6:]
    assemble_into(new_ref, to_ref, *refs[5:9])
    assemble_into(other_ref, to_ref, *refs[9:13])
    product_kernel(refs[:5], new_ref, other_ref, *term_refs)


def products(kernel, scalars, row_parts, weights, after=()):
    term = jax.ShapeDtypeStruct((2, 2, 128, 512), jnp.bfloat16)
    own = jax.ShapeDtypeStruct((512, 1024), jnp.bfloat16)
    vmem = pl.BlockSpec(memory_space=pltpu.VMEM)
    arrays = (*scalars, *row_parts, *weights)
    return pl.pallas_call(
        lambda *refs: kernel(*refs[: len(arrays)], *refs[-6:]),
        in_specs=[pl.BlockSpec(memory_space=pltpu.SMEM)] * len(scalars)
        + [vmem] * (len(arrays) - len(scalars))
        + [pl.BlockSpec(memory_space=pl.ANY)] * len(after),
        out_specs=[vmem] * 5,
        out_shape=[term] * 4 + [own],
        scratch_shapes=[pltpu.VMEM(own.shape, own.dtype)],
        compiler_params=pltpu.CompilerParams(vmem_limit_bytes=20 * 2**20),
        cost_estimate=BRIEF,
        name="products",
    )(*arrays, *after)


def add(kept, arrived):
    return kept.astype(jnp.float32) + arrived.astype(jnp.float32)


def over_z(parts):
    return [parts[0]] + [lax.ppermute(parts[k], "mp", mp_swap(0, k)) for k in (1, 2, 3)]


def over_y(parts):
    return [parts[0]] + [lax.ppermute(parts[k], "mp", mp_swap(k, 0)) for k in (1, 2, 3)]


def over_y_ring(column):
    near = [lax.ppermute(column, "mp", mp_swap(k, 0)) for k in (1, 2)]
    far = [
        lax.ppermute(near[0][:4], "mp", mp_swap(2, 0)),
        lax.ppermute(near[1][4:], "mp", mp_swap(1, 0)),
    ]
    return [column, *near, *far]


def swap_core(own, cuts):
    return [
        lax.ppermute(piece, "dp", dp_swap(0, 0, 1)) for piece in jnp.split(own, cuts)
    ]


def first_sums(parts):
    send_a, keep_a, send_b, keep_b = parts
    got_a = lax.ppermute(send_a, "dp", dp_swap(1, 0, 0))
    got_b = lax.ppermute(send_b, "dp", dp_swap(2, 0, 0))
    sends = [add(k[1], g[1]).astype(jnp.bfloat16) for k, g in ((keep_a, got_a), (keep_b, got_b))]
    return sends, [add(keep_a[0], got_a[0]), add(keep_b[0], got_b[0])]


def second_sums(sends, keeps):
    got_a = lax.ppermute(sends[0], "dp", dp_swap(2, 0, 0))
    got_b = lax.ppermute(sends[1], "dp", dp_swap(1, 0, 0))
    return jnp.concatenate([add(keeps[0], got_a), add(keeps[1], got_b)], axis=-1)


def last_sum(both):
    return add(both[0], lax.ppermute(both[1].astype(jnp.bfloat16), "dp", dp_swap(0, 1, 0)))


def local(
    weight_gate,
    weight_up,
    grad_gate,
    grad_up,
    moment_gate,
    moment_up,
    second_gate,
    second_up,
    layer_input,
    queries,
    fresh_keys,
    fresh_values,
    cached_keys,
    cached_values,
    lengths,
    norm_gain,
):
    dp = lax.axis_index("dp")
    mp = lax.axis_index("mp")
    x, z_hi, core = dp // 4, dp // 2 % 2, dp % 2
    y, z_lo = mp // 4, mp % 4
    gray_x, gray_y = x ^ (x >> 1), y ^ (y >> 1)

    def place(gray):
        return gray ^ (gray >> 1)

    to = jnp.stack(
        [place(gray_x ^ flip) * 2 + (z_hi ^ flip_z) for flip in range(4) for flip_z in range(2)]
        + [core]
        + [place(gray_y ^ flip) for flip in range(4)]
        + [z_lo]
    ).astype(jnp.int32)

    gate_step = adam_places(weight_gate, grad_gate, moment_gate, second_gate)
    gate_step, lengths = lax.optimization_barrier((gate_step, lengths))
    gate_own = lax.all_to_all(gate_step, "mp", split_axis=0, concat_axis=0, tiled=True)
    gate_own = gate_own.reshape(512, 1024)

    by_x = attend(
        to, lengths, queries, layer_input, fresh_keys, fresh_values, cached_keys, cached_values,
        norm_gain.reshape(1, D),
    )
    by_x, weight_up = lax.optimization_barrier((by_x, weight_up))
    up_parts = adam_flips(to, weight_up, grad_up, moment_up, second_up)
    by_x, up_parts = lax.optimization_barrier((by_x, up_parts))
    up_parts = over_y(up_parts)
    by_x = [by_x[0]] + [lax.ppermute(by_x[k], "dp", dp_swap(k, 0, 0)) for k in (1, 2, 3)]
    here, there = swap_axes(by_x)
    spread = interleave(here, lax.ppermute(there, "dp", dp_swap(0, 1, 0)))
    along_z = over_z([spread] * 4)
    column, up_parts, gate_own = lax.optimization_barrier(
        (join_rows(along_z), up_parts, gate_own)
    )
    gate_other = swap_core(gate_own, (176, 352))
    row_parts = over_y_ring(column)
    up_parts = over_z(regroup(up_parts))
    *gate_terms, gate_new = products(
        first_kernel, (), row_parts, (gate_own, *gate_other), up_parts[1:3]
    )
    gate_new, up_parts[3] = lax.optimization_barrier((gate_new, up_parts[3]))
    up_other = [swap_core(part, ())[0] for part in up_parts]
    *up_terms, up_new = products(second_kernel, (to,), row_parts, (*up_parts, *up_other))

    gate_terms[1], gate_terms[3], up_new = lax.optimization_barrier(
        (gate_terms[1], gate_terms[3], up_new)
    )
    gate_sends, gate_keeps = first_sums(gate_terms)
    gate_sends, up_terms = lax.optimization_barrier((gate_sends, up_terms))
    gate_both = second_sums(gate_sends, gate_keeps)
    up_both = second_sums(*first_sums(up_terms))
    gate_total, up_both = lax.optimization_barrier((last_sum(gate_both), up_both))
    up_total = last_sum(up_both)
    hidden = (jax.nn.silu(gate_total) * up_total).astype(jnp.bfloat16)

    row = jnp.arange(128)
    y_flip, z_flip, step_at, row_at = row // 32, row // 8 % 4, row // 2 % 4, row % 2
    target = step_at * 32 + (place(gray_y ^ y_flip) * 4 + (z_lo ^ z_flip)) * 2 + row_at
    placed = (row[:, None] == target[None, :]).astype(jnp.bfloat16)
    hidden = jnp.dot(placed, hidden, preferred_element_type=jnp.float32).astype(jnp.bfloat16)
    return gate_new, up_new, hidden.reshape(STEPS, 32, 1024)


def solution(mesh):
    rows = P(("dp", "mp"), None)
    steps = P(None, ("dp", "mp"), None)
    cache = P(("dp", "mp"), None, None)
    in_specs = (rows,) * 8 + (steps,) * 4 + (cache,) * 2 + (P(("dp", "mp")), P())
    out_specs = (P("dp", "mp"), P("dp", "mp"), P(None, "dp", "mp"))
    return jax.shard_map(local, mesh=mesh, in_specs=in_specs, out_specs=out_specs, check_vma=False)
```
